32 devices in a mesh: grp: 4 (over y, x), pts: 8 (over z, core).
Axes of the slice: x: 2, y: 2, z: 4, core: 2. Of those that a mesh axis runs over, the one named last changes fastest.
Arguments:
- points: bfloat16 [32768, 512], P(('grp', 'pts')), may hold values from -16 to 16
- ball_ids: int32 [64, 512], P(('grp', 'pts')), may hold values from 0 to 3, never falling along the last dimension, each value on 1 to 256 neighbouring positions
- send_pick: int32 [32, 8], P(('grp', 'pts')), may hold values from 0 to 8, as said below
- recv_from: int32 [32, 8], P(('grp', 'pts')), may hold values from 0 to 7, as said below
- gain_one: float32 [512], replicated, may hold values from 0.1 to 1.9
- attn_in_one: bfloat16 [512, 1536], replicated, may hold values from -2 to 2
- attn_out_one: bfloat16 [512, 512], replicated, may hold values from -0.25 to 0.25
- gain_two: float32 [512], replicated, may hold values from 0.1 to 1.9
- mlp_up: bfloat16 [512, 2048], replicated, may hold values from -0.25 to 0.25
- mlp_down: bfloat16 [2048, 512], replicated, may hold values from -0.125 to 0.125
- gain_three: float32 [512], replicated, may hold values from 0.1 to 1.9
- compress_proj: bfloat16 [512, 1024], replicated, may hold values from -2 to 2
- attn_in_two: bfloat16 [512, 1536], replicated, may hold values from -2 to 2
- attn_out_two: bfloat16 [512, 512], replicated, may hold values from -0.25 to 0.25
Outputs:
- second: bfloat16 [32768, 512], P(('grp', 'pts'))
The draws below stay inside these ranges and needn't reach their ends.
Inputs may be any that keep to these rules, and one draw needn't show every extreme that they name: `send_pick`: slot q + c of device d goes to the device of pts index q in d's grp row; an entry is the local leaf block sent there, or 8 for an empty slot; each of a device's 8 blocks stands in exactly one slot, and every device receives exactly 8 blocks. `recv_from`: entry j of row d is the received slot p + c (p the sender's pts index in d's grp row, c its slot toward d) that fills rotated position j; a row's entries are distinct and are exactly the non-empty slots that device d receives according to send_pick.
All inputs are finite; a program needn't handle non-finite values.
Results may differ from the reference program's by a relative error of at most 0.017.
The reference program's roundings to bfloat16 on the way count: a program that leaves them out, or rounds other values in their place, can miss the bound.
Values may be sent and summed in bfloat16 or wider, within the bound.
No kernel may reach another device: no remote copies, remote signals or barrier semaphores. Data moves between devices by JAX's collectives and lax.ppermute only.
A program may use at most 128 MiB of HBM per device.

```python
import math
import jax
import jax.numpy as jnp
import numpy as np
from jax import lax

D = 512
HEADS = 8
HEAD = 64
INNER = 2048
LEAF = 128
BALL = 512
CMP = 256
PTS_DEV = 1024
BLOCKS_DEV = 8
PEERS = 8
CAP = 1
SLOTS = 8
TOTAL = 32768
BALLS = 64
BLOCKS = 256
COMP = 128
DEVICES = 32


def slab_plan(slab_key):
    subkeys = jax.random.split(slab_key, 4)
    relabel = jax.random.permutation(subkeys[0], PEERS).astype(jnp.int32)
    offsets = jax.random.permutation(subkeys[1], SLOTS)[:BLOCKS_DEV].astype(jnp.int32)
    senders = jnp.arange(PEERS, dtype=jnp.int32)[:, None]
    receiver = relabel[(senders + offsets[None, :]) % PEERS]
    column = jnp.broadcast_to(offsets[None, :] // PEERS, receiver.shape)

    def shuffled(one_key):
        return jax.random.permutation(one_key, BLOCKS_DEV).astype(jnp.int32)
    blocks = jax.vmap(shuffled)(jax.random.split(subkeys[2], PEERS))
    send_slot = receiver * CAP + column
    sender_rows = jnp.broadcast_to(senders, send_slot.shape)
    send_table = jnp.full((PEERS, SLOTS), BLOCKS_DEV, jnp.int32).at[sender_rows, send_slot].set(blocks)
    arrival = sender_rows * CAP + column
    arrival_order = jnp.argsort(receiver.reshape(-1), stable=True)
    grouped = arrival.reshape(-1)[arrival_order].reshape(PEERS, BLOCKS_DEV)
    mixing = jax.vmap(shuffled)(jax.random.split(subkeys[3], PEERS))
    recv_table = jnp.take_along_axis(grouped, mixing, axis=1)
    return (send_table, recv_table)


def leaf_plan(key):
    plan_key = jax.random.fold_in(key, 4242)
    slab_keys = jax.random.split(plan_key, DEVICES // PEERS)
    send_table, recv_table = jax.vmap(slab_plan)(slab_keys)
    return (send_table.reshape(DEVICES, SLOTS), recv_table.reshape(DEVICES, BLOCKS_DEV))


def draw_send_pick(key, part):
    return leaf_plan(key)[0]


def draw_recv_from(key, part):
    return leaf_plan(key)[1]


def draw_points(key, part):
    noise = jax.random.normal(jax.random.fold_in(key, 11), (TOTAL, D), jnp.float32)
    return jnp.clip(noise, -6.0, 6.0).astype(jnp.bfloat16)


def draw_attn_in_one(key, part):
    base = jax.random.normal(jax.random.fold_in(key, 21), (D, 3 * D), jnp.float32) * D ** (-0.5)
    return jnp.clip(base, -2.0, 2.0).astype(jnp.bfloat16)


def draw_attn_in_two(key, part):
    base = jax.random.normal(jax.random.fold_in(key, 31), (D, 3 * D), jnp.float32) * D ** (-0.5)
    return jnp.clip(base, -2.0, 2.0).astype(jnp.bfloat16)


def draw_compress_proj(key, part):
    base = jax.random.normal(jax.random.fold_in(key, 41), (D, 2 * D), jnp.float32) * D ** (-0.5)
    return jnp.clip(base, -2.0, 2.0).astype(jnp.bfloat16)


def profile(number_of, total, most, lean):
    portions = [(1 << 20) // math.isqrt(rank ** lean) + 1 for rank in range(2, number_of + 1)]
    spare, holding = total - most - (number_of - 1), [1] * (number_of - 1)
    while spare > 0:
        movable = [i for i in range(number_of - 1) if holding[i] < most]
        whole, budget = sum([portions[i] for i in movable]), spare
        for i in movable:
            more = min(most - holding[i], max(1, budget * portions[i] // whole), spare)
            holding[i] = holding[i] + more
            spare = spare - more
    return np.array([most] + holding)


def uneven_parts(rng, amount, total, limit, slope):
    if amount == 2:
        one = jax.random.randint(rng, (), max(1, total - limit), min(limit, total - 1) + 1)
        return jnp.stack([one, total - one])
    tallies = jnp.asarray(profile(amount, total, limit, slope), jnp.int32)
    twos = (amount - 1) // 2
    giver, taker = tallies[1:1 + 2 * twos:2], tallies[2:2 + 2 * twos:2]
    margin = jnp.minimum(giver - 1, limit - taker)
    passed = jax.random.randint(jax.random.fold_in(rng, 1), (twos,), 0, 1 << 20) % (margin + 1)
    tallies = tallies.at[1:1 + 2 * twos:2].set(giver - passed).at[2:2 + 2 * twos:2].set(taker + passed)
    return tallies[jax.random.permutation(jax.random.fold_in(rng, 2), amount)]


def normal_values(key, extent, scale, most, held_as=jnp.bfloat16):
    values = scale * jax.random.normal(key, extent, jnp.float32)
    return jnp.clip(values, min=-most, max=most).astype(held_as)


def setup_inputs(seed: int = 0) -> dict:
    keys = jax.random.split(jax.random.key(seed), 15)
    return {
        "points": draw_points(jax.random.fold_in(keys[14], 71), 0),
        "ball_ids": jax.vmap(lambda own: jnp.searchsorted(jnp.cumsum(uneven_parts(own, 4, BALL, BALL // 2, 2)), jnp.arange(BALL), side="right"))(jax.random.split(keys[1], BALLS)).reshape((BALLS, BALL)).astype(jnp.int32),
        "send_pick": draw_send_pick(jax.random.fold_in(keys[14], 71), 0),
        "recv_from": draw_recv_from(jax.random.fold_in(keys[14], 71), 0),
        "gain_one": jnp.clip(1.0 + 0.18 * jax.random.normal(keys[4], (D,), jnp.float32), 0.1, 1.9),
        "attn_in_one": draw_attn_in_one(jax.random.fold_in(keys[14], 71), 0),
        "attn_out_one": normal_values(keys[6], (D, D), D ** -0.5, 0.25),
        "gain_two": jnp.clip(1.0 + 0.18 * jax.random.normal(keys[7], (D,), jnp.float32), 0.1, 1.9),
        "mlp_up": normal_values(keys[8], (D, INNER), D ** -0.5, 0.25),
        "mlp_down": normal_values(keys[9], (INNER, D), INNER ** -0.5, 0.125),
        "gain_three": jnp.clip(1.0 + 0.18 * jax.random.normal(keys[10], (D,), jnp.float32), 0.1, 1.9),
        "compress_proj": draw_compress_proj(jax.random.fold_in(keys[14], 71), 0),
        "attn_in_two": draw_attn_in_two(jax.random.fold_in(keys[14], 71), 0),
        "attn_out_two": normal_values(keys[13], (D, D), D ** -0.5, 0.25),
    }


def norm_rows(values, gain):
    wide = values.astype(jnp.float32)
    return wide * lax.rsqrt(lax.optimization_barrier(jnp.mean(wide * wide, axis=-1, keepdims=True)) + 1e-06) * gain

def softmax_rows(scores):
    top = lax.optimization_barrier(jnp.max(scores, axis=-1, keepdims=True))
    expo = jnp.exp(scores - top)
    return expo / lax.optimization_barrier(jnp.sum(expo, axis=-1, keepdims=True))

def first_ball(packed):
    rows, member = packed
    queries = rows[:, 0].astype(jnp.float32)
    key_rows = rows[:, 1].astype(jnp.float32)
    scores = jnp.einsum('qhd,khd->hqk', queries, key_rows) * HEAD ** (-0.5)
    same_ball = member[:, None] == member[None, :]
    scores = jnp.where(same_ball[None], scores, -1e+30)
    weights = softmax_rows(scores).astype(jnp.bfloat16)
    mixed = jnp.einsum('hqk,khd->qhd', weights.astype(jnp.float32), rows[:, 2].astype(jnp.float32))
    return mixed.astype(jnp.bfloat16).reshape(rows.shape[0], D)

def second_ball(rows, comp_keys, comp_values):
    queries = rows[:, 0].astype(jnp.float32)
    scores = jnp.einsum('qhd,khd->hqk', queries, rows[:, 1].astype(jnp.float32)) * HEAD ** (-0.5)
    weights = softmax_rows(scores).astype(jnp.bfloat16)
    local_out = jnp.einsum('hqk,khd->qhd', weights.astype(jnp.float32), rows[:, 2].astype(jnp.float32))
    comp_scores = jnp.einsum('qhd,khd->hqk', queries, comp_keys.astype(jnp.float32)) * HEAD ** (-0.5)
    comp_weights = softmax_rows(comp_scores).astype(jnp.bfloat16)
    comp_out = jnp.einsum('hqk,khd->qhd', comp_weights.astype(jnp.float32), comp_values.astype(jnp.float32))
    return (local_out + comp_out).astype(jnp.bfloat16).reshape(rows.shape[0], D)

def layer_first(packed, gain_one, attn_in_one, attn_out_one, gain_two, mlp_up, mlp_down, gain_three):
    points, member = packed
    count = points.shape[0]
    normed = norm_rows(points, gain_one).astype(jnp.bfloat16)
    proj = jnp.dot(normed, attn_in_one, preferred_element_type=jnp.float32).astype(jnp.bfloat16)
    proj = proj.reshape(count // BALL, BALL, 3, HEADS, HEAD)
    mixed = lax.map(first_ball, (proj, member)).reshape(count, D)
    middle = (points.astype(jnp.float32) + jnp.dot(mixed, attn_out_one, preferred_element_type=jnp.float32)).astype(jnp.bfloat16)
    inner = norm_rows(middle, gain_two).astype(jnp.bfloat16)
    hidden = jax.nn.gelu(jnp.dot(inner, mlp_up, preferred_element_type=jnp.float32)).astype(jnp.bfloat16)
    layer_one = (middle.astype(jnp.float32) + jnp.dot(hidden, mlp_down, preferred_element_type=jnp.float32)).astype(jnp.bfloat16)
    normed_two = norm_rows(layer_one, gain_three).astype(jnp.bfloat16)
    pooled = (lax.optimization_barrier(jnp.sum(normed_two.reshape(count // CMP, CMP, D).astype(jnp.float32), axis=1)) * CMP ** (-0.5)).astype(jnp.bfloat16)
    return (layer_one, normed_two, pooled)

def reference(points, ball_ids, send_pick, recv_from, gain_one, attn_in_one, attn_out_one, gain_two, mlp_up, mlp_down, gain_three, compress_proj, attn_in_two, attn_out_two):

    def run_first(packed):
        return layer_first(packed, gain_one, attn_in_one, attn_out_one, gain_two, mlp_up, mlp_down, gain_three)
    layer_one, normed_two, pooled = lax.map(run_first, (points.reshape(DEVICES, PTS_DEV, D), ball_ids.reshape(DEVICES, PTS_DEV // BALL, BALL)))
    layer_one = layer_one.reshape(TOTAL, D)
    normed_two = normed_two.reshape(TOTAL, D)
    pooled = pooled.reshape(COMP, D)
    comp = jnp.dot(pooled, compress_proj, preferred_element_type=jnp.float32).astype(jnp.bfloat16)
    comp_keys = comp[:, :D].reshape(COMP, HEADS, HEAD)
    comp_values = comp[:, D:].reshape(COMP, HEADS, HEAD)
    device = jnp.arange(DEVICES, dtype=jnp.int32)[:, None]
    source_peer = recv_from // CAP
    column = recv_from % CAP
    sender = device // PEERS * PEERS + source_peer
    block = send_pick[sender, device % PEERS * CAP + column]
    order = (sender * BLOCKS_DEV + block).reshape(-1).astype(jnp.int32)
    rotated_z = layer_one.reshape(BLOCKS, LEAF, D)[order].reshape(TOTAL, D)
    rotated_h = normed_two.reshape(BLOCKS, LEAF, D)[order].reshape(TOTAL, D)

    def run_second(packed):
        zrows, hrows = packed
        proj = jnp.dot(hrows, attn_in_two, preferred_element_type=jnp.float32).astype(jnp.bfloat16)
        proj = proj.reshape(PTS_DEV // BALL, BALL, 3, HEADS, HEAD)
        branch = lax.map(lambda rows: second_ball(rows, comp_keys, comp_values), proj).reshape(PTS_DEV, D)
        return (zrows.astype(jnp.float32) + jnp.dot(branch, attn_out_two, preferred_element_type=jnp.float32)).astype(jnp.bfloat16)
    result = lax.map(run_second, (rotated_z.reshape(DEVICES, PTS_DEV, D), rotated_h.reshape(DEVICES, PTS_DEV, D)))
    placed = jnp.zeros((BLOCKS, LEAF, D), jnp.bfloat16).at[order].set(result.reshape(BLOCKS, LEAF, D))
    return placed.reshape(TOTAL, D)
```

```python
from functools import partial
import math

import jax
import jax.numpy as jnp
from jax import lax
from jax.experimental import pallas as pl
from jax.experimental.pallas import tpu as pltpu
from jax.sharding import PartitionSpec as P

HEAD = 64
LEAF = 128
BALL = 512
CMP = 256
PAIR = 2 * HEAD
AUG = HEAD + 16
HIDE = 512
MIB = 1 << 20
F32 = jnp.float32
BF16 = jnp.bfloat16
SCALE = HEAD ** (-0.5) * math.log2(math.e)

ANY = pl.BlockSpec(memory_space=pl.ANY)
VMEM = pl.BlockSpec(memory_space=pltpu.VMEM)
SMEM = pl.BlockSpec(memory_space=pltpu.SMEM)


def norm(values, gain):
    wide = values.astype(F32)
    return wide * lax.rsqrt(jnp.mean(wide * wide, axis=-1, keepdims=True) + 1e-06) * gain


def gelu(x):
    c = math.sqrt(2.0 / math.pi)
    t = jnp.tanh(x * (c + (c * 0.044715) * (x * x)))
    return x * (0.5 + 0.5 * t)


def dot(a, b):
    return jnp.dot(a, b, preferred_element_type=F32)


def dot_t(a, b):
    return lax.dot_general(a, b, (((1,), (1,)), ((), ())), preferred_element_type=F32)


def aligned(index, size):
    return pl.ds(pl.multiple_of(index * size, size), size)


def head_keys(keys, half):
    lane = lax.broadcasted_iota(jnp.int32, keys.shape, 1)
    return jnp.where((lane >= HEAD) == bool(half), keys, jnp.zeros_like(keys))


def softmax_mix(scores, values_aug):
    top = jnp.max(scores, axis=0, keepdims=True)
    expo = jnp.exp2(scores - top).astype(BF16)
    mixed = dot(values_aug, expo)
    return mixed[:HEAD] * (1.0 / mixed[HEAD : HEAD + 1])


def send_to(me, s, peers):
    return me ^ s if peers & (peers - 1) == 0 else (me + s) % peers


def got_from(me, s, peers):
    return me ^ s if peers & (peers - 1) == 0 else (me + peers - s) % peers


def layer_one_kernel(peers, cap, slots, late, *refs):
    n_in = 13 if late else 12
    ins, rest = refs[:n_in], refs[n_in:]
    me_ref, pick_ref, points, ids, gain1, w_in, w_out, gain2, w_up, w_down, gain3 = ins[:11]
    lead = ins[11]
    h_first = ins[12] if late else None
    z_out, pool_out = rest[:2]
    n_send = len(slots)
    sends = rest[2 : 2 + n_send]
    rest = rest[2 + n_send :]
    if not late:
        h_out = rest[0]
        rest = rest[1:]
    (x_s, win_s, wout_s, wup_s, wdown_s, q_s, k_s, va_s, bias_s, mix_s, y_s, h_s, sem) = rest
    per = BALL // LEAF
    first = lead[0]
    ball = (1 - first) if late else first
    rows = aligned(ball, BALL)
    copies = [
        pltpu.make_async_copy(points.at[rows, :], x_s, sem.at[0]),
        pltpu.make_async_copy(w_in, win_s, sem.at[1]),
        pltpu.make_async_copy(w_out, wout_s, sem.at[2]),
        pltpu.make_async_copy(w_up, wup_s, sem.at[3]),
        pltpu.make_async_copy(w_down, wdown_s, sem.at[4]),
    ]
    for copy in copies:
        copy.start()
    width = x_s.shape[1]
    heads = width // HEAD

    own = ids[pl.ds(ball, 1), :]
    across = jnp.broadcast_to(own, (LEAF, BALL)).astype(F32)
    down = across.T
    for c in range(BALL // LEAF):
        cols = slice(c * LEAF, (c + 1) * LEAF)
        bias_s[:, cols] = jnp.where(down == across[:1, cols], 0.0, -1e30)
    for h in range(heads):
        va_s[h, HEAD:, :] = jnp.ones((AUG - HEAD, BALL), BF16)

    copies[0].wait()
    h1 = norm(x_s[...], gain1[...]).astype(BF16)
    copies[1].wait()
    q_s[...] = (dot(h1, win_s[:, :width]) * SCALE).astype(BF16)
    k_s[...] = dot(h1, win_s[:, width : 2 * width]).astype(BF16)
    values = dot(h1, win_s[:, 2 * width :]).astype(BF16).T
    for h in range(heads):
        va_s[h, :HEAD, :] = values[h * HEAD : (h + 1) * HEAD]

    @pl.loop(0, heads // 2)
    def _(pair):
        cols = aligned(pair, PAIR)
        q, k = q_s[:, cols], k_s[:, cols]
        for half in range(2):
            scores = dot_t(head_keys(k, half), q) + bias_s[...]
            out = softmax_mix(scores, va_s[2 * pair + half])
            mix_s[aligned(2 * pair + half, HEAD), :] = out.astype(BF16)

    copies[2].wait()
    y = (x_s[...].astype(F32) + dot(mix_s[...].T, wout_s[...])).astype(BF16)
    y_s[...] = y
    inner = norm(y, gain2[...]).astype(BF16)
    copies[3].wait()
    copies[4].wait()
    total = jnp.zeros((BALL, width), F32)
    for c in range(wup_s.shape[1] // HIDE):
        cols = slice(c * HIDE, (c + 1) * HIDE)
        hidden = gelu(dot(inner, wup_s[:, cols])).astype(BF16)
        total = total + dot(hidden, wdown_s[cols, :])
    z = (y_s[...].astype(F32) + total).astype(BF16)
    z_out[...] = z
    h3 = norm(z, gain3[...]).astype(BF16)
    h_s[...] = h3
    wide = h3.astype(F32)
    for c in range(BALL // CMP):
        part = jnp.sum(wide[c * CMP : (c + 1) * CMP], axis=0, keepdims=True) * CMP ** (-0.5)
        pool_out[c : c + 1, :] = part.astype(BF16)
    if not late:
        h_out[...] = h3
    me = me_ref[0]
    for s, send in zip(slots, sends):
        for c in range(cap):
            block = jnp.minimum(pick_ref[0, send_to(me, s, peers) * cap + c], 2 * per - 1)
            place = aligned(lax.rem(block, per), LEAF)
            at = slice(c * LEAF, (c + 1) * LEAF)
            if late:
                here = block // per == ball

                @pl.when(here)
                def _():
                    send[at, :] = h_s[place, :]

                @pl.when(jnp.logical_not(here))
                def _():
                    send[at, :] = h_first[place, :]

            else:
                send[at, :] = h_s[place, :]


def layer_one(peers, cap, slots, late, me, pick, points, ids, weights, lead, h_first=None):
    width = points.shape[1]
    hidden = weights[4].shape[1]
    half = jax.ShapeDtypeStruct((BALL, width), BF16)
    block = jax.ShapeDtypeStruct((cap * LEAF, width), BF16)
    outs = [half, jax.ShapeDtypeStruct((BALL // CMP, width), BF16)] + [block] * len(slots)
    specs = [SMEM, SMEM, ANY, VMEM, VMEM, ANY, ANY, VMEM, ANY, ANY, VMEM, SMEM]
    args = [me, pick, points, ids, *weights, lead]
    if late:
        specs.append(VMEM)
        args.append(h_first)
    else:
        outs.append(half)
    heads = width // HEAD
    return pl.pallas_call(
        partial(layer_one_kernel, peers, cap, slots, late),
        out_shape=outs,
        in_specs=specs,
        out_specs=[VMEM] * len(outs),
        scratch_shapes=[
            pltpu.VMEM((BALL, width), BF16),
            pltpu.VMEM((width, 3 * width), BF16),
            pltpu.VMEM((width, width), BF16),
            pltpu.VMEM((width, hidden), BF16),
            pltpu.VMEM((hidden, width), BF16),
            pltpu.VMEM((BALL, width), BF16),
            pltpu.VMEM((BALL, width), BF16),
            pltpu.VMEM((heads, AUG, BALL), BF16),
            pltpu.VMEM((BALL, BALL), F32),
            pltpu.VMEM((width, BALL), BF16),
            pltpu.VMEM((BALL, width), BF16),
            pltpu.VMEM((BALL, width), BF16),
            pltpu.SemaphoreType.DMA((5,)),
        ],
        compiler_params=pltpu.CompilerParams(vmem_limit_bytes=32 * MIB),
        cost_estimate=pl.CostEstimate(
            flops=2 * BALL * width * (4 * width + 2 * hidden) + 16 * BALL * BALL * width,
            bytes_accessed=8 * MIB,
            transcendentals=heads * BALL * BALL,
        ),
        name="layer_one_late" if late else "layer_one_lead",
    )(*args)


def place_of(recv_ref, slot, blocks):
    place, found = jnp.int32(0), jnp.int32(0)
    for j in range(blocks):
        hit = (recv_ref[0, j] == slot).astype(jnp.int32)
        place = place + j * hit
        found = found + hit
    return place, found > 0


def layer_two_kernel(peers, cap, blocks, *refs):
    me_ref, recv_ref = refs[:2]
    arrived = refs[2 : 2 + peers]
    pooled, w_comp, w_in = refs[2 + peers : 5 + peers]
    outs = refs[5 + peers : 5 + 2 * peers]
    q_s, k_s, va_s, ck_s, cv_s, mix_s, a_s = refs[5 + 2 * peers :]
    width = q_s.shape[1]
    heads = width // HEAD
    me = me_ref[0]
    comp = pooled.shape[0]
    for h in range(heads):
        va_s[h, HEAD:, :] = jnp.ones((AUG - HEAD, va_s.shape[2]), BF16)
        cv_s[h, HEAD:, :] = jnp.ones((AUG - HEAD, comp), BF16)
    ck_s[...] = dot(pooled[...], w_comp[:, :width]).astype(BF16)
    values = dot(pooled[...], w_comp[:, width:]).astype(BF16).T
    for h in range(heads):
        cv_s[h, :HEAD, :] = values[h * HEAD : (h + 1) * HEAD]
    for s in range(peers):
        for c in range(cap):
            place, found = place_of(recv_ref, got_from(me, s, peers) * cap + c, blocks)

            @pl.when(found)
            def _():
                block = arrived[s][c * LEAF : (c + 1) * LEAF, :]
                rows = aligned(place, LEAF)
                q_s[rows, :] = (dot(block, w_in[:, :width]) * SCALE).astype(BF16)
                k_s[rows, :] = dot(block, w_in[:, width : 2 * width]).astype(BF16)
                values = dot(block, w_in[:, 2 * width :]).astype(BF16).T
                for h in range(heads):
                    va_s[h, :HEAD, rows] = values[h * HEAD : (h + 1) * HEAD]

    for ball in range(blocks * LEAF // BALL):
        rows = slice(ball * BALL, (ball + 1) * BALL)

        @pl.loop(0, heads // 2)
        def _(pair):
            cols = aligned(pair, PAIR)
            q, k, ck = q_s[rows, cols], k_s[rows, cols], ck_s[:, cols]
            for half in range(2):
                h = 2 * pair + half
                out = softmax_mix(dot_t(head_keys(k, half), q), va_s[h, :, rows])
                far = softmax_mix(dot_t(head_keys(ck, half), q), cv_s[h])
                mix_s[aligned(h, HEAD), :] = (out + far).astype(BF16)

        a_s[rows, :] = mix_s[...].T
    for s in range(peers):
        for c in range(cap):
            place, _ = place_of(recv_ref, got_from(me, s, peers) * cap + c, blocks)
            outs[s][c * LEAF : (c + 1) * LEAF, :] = a_s[aligned(place, LEAF), :]


def layer_two(peers, cap, me, recv, arrived, pooled, w_comp, w_in):
    blocks = recv.shape[1]
    width = w_in.shape[0]
    heads = width // HEAD
    rows = blocks * LEAF
    comp = pooled.shape[0]
    block = jax.ShapeDtypeStruct((cap * LEAF, width), BF16)
    return pl.pallas_call(
        partial(layer_two_kernel, peers, cap, blocks),
        out_shape=[block] * peers,
        in_specs=[SMEM, SMEM] + [VMEM] * (peers + 3),
        out_specs=[VMEM] * peers,
        scratch_shapes=[
            pltpu.VMEM((rows, width), BF16),
            pltpu.VMEM((rows, width), BF16),
            pltpu.VMEM((heads, AUG, rows), BF16),
            pltpu.VMEM((comp, width), BF16),
            pltpu.VMEM((heads, AUG, comp), BF16),
            pltpu.VMEM((width, BALL), BF16),
            pltpu.VMEM((rows, width), BF16),
        ],
        compiler_params=pltpu.CompilerParams(vmem_limit_bytes=32 * MIB),
        name="layer_two",
    )(me, recv, *arrived, pooled, w_comp, w_in)


def final_kernel(peers, cap, me_ref, pick_ref, lead, *refs):
    back = refs[:peers]
    w_out, z_first, z_late, out = refs[peers:]
    per = BALL // LEAF
    me = me_ref[0]
    for s in range(peers):
        for c in range(cap):
            block = pick_ref[0, send_to(me, s, peers) * cap + c]

            @pl.when(block < 2 * per)
            def _():
                place = aligned(lax.rem(block, per), LEAF)
                early = block // per == lead[0]
                z = jnp.where(early, z_first[place, :], z_late[place, :]).astype(F32)
                gain = dot(back[s][c * LEAF : (c + 1) * LEAF, :], w_out[...])
                out[aligned(block, LEAF), :] = (z + gain).astype(BF16)


def final(peers, cap, me, pick, lead, back, w_out, z_first, z_late):
    rows = 2 * z_first.shape[0]
    return pl.pallas_call(
        partial(final_kernel, peers, cap),
        out_shape=jax.ShapeDtypeStruct((rows, z_first.shape[1]), BF16),
        in_specs=[SMEM] * 3 + [VMEM] * (peers + 3),
        out_specs=VMEM,
        compiler_params=pltpu.CompilerParams(vmem_limit_bytes=24 * MIB),
        name="last_product",
    )(me, pick, lead, *back, w_out, z_first, z_late)


def gather_all(rows, axes):
    for axis, size in axes:
        if size & (size - 1):
            rows = lax.all_gather(rows, axis, axis=0, tiled=True)
            continue
        bit = 1
        while bit < size:
            pattern = [(i, i ^ bit) for i in range(size)]
            rows = jnp.concatenate([rows, lax.ppermute(rows, axis, pattern)])
            bit *= 2
    return rows


def shards(
    axes,
    points,
    ball_ids,
    send_pick,
    recv_from,
    gain_one,
    attn_in_one,
    attn_out_one,
    gain_two,
    mlp_up,
    mlp_down,
    gain_three,
    compress_proj,
    attn_in_two,
    attn_out_two,
):
    peers = axes[1][1]
    cap = send_pick.shape[1] // peers
    per = BALL // LEAF
    me = lax.axis_index("pts").astype(jnp.int32)
    far = peers - 1
    target = send_to(me, far, peers)
    lead_slot = lax.dynamic_slice(send_pick[0], (target * cap,), (1,))
    lead = jnp.minimum(lead_slot // per, ball_ids.shape[0] - 1).astype(jnp.int32)
    me1 = me.reshape(1)
    weights = (
        gain_one.reshape(1, -1),
        attn_in_one,
        attn_out_one,
        gain_two.reshape(1, -1),
        mlp_up,
        mlp_down,
        gain_three.reshape(1, -1),
    )
    one = partial(layer_one, peers, cap)
    early = [far] if cap == 1 else []
    z_first, pool_first, *lead_sends, h_first = one(
        early, False, me1, send_pick, points, ball_ids, weights, lead
    )
    order = [s for s in range(peers - 1, -1, -1) if s not in early]
    z_late, pool_late, *late_sends = one(
        order, True, me1, send_pick, points, ball_ids, weights, lead, h_first
    )
    sends = dict(zip(early + order, lead_sends + late_sends))

    def travel(blocks, s, home):
        if s == 0:
            return blocks
        pattern = [(i, send_to(i, s, peers)) for i in range(peers)]
        if home:
            pattern = [(b, a) for a, b in pattern]
        return lax.ppermute(blocks, "pts", pattern)

    arrived = {s: travel(sends[s], s, False) for s in early + order}
    pooled = gather_all(jnp.concatenate([pool_first, pool_late]), axes)
    mixed = layer_two(
        peers, cap, me1, recv_from, [arrived[s] for s in range(peers)], pooled, compress_proj, attn_in_two
    )
    back = {s: travel(mixed[s], s, True) for s in range(peers - 1, -1, -1)}
    return final(
        peers,
        cap,
        me1,
        send_pick,
        lead,
        [back[s] for s in range(peers)],
        attn_out_two,
        z_first,
        z_late,
    )


def solution(mesh):
    rows = P(("grp", "pts"), None)
    axes = (("grp", mesh.shape["grp"]), ("pts", mesh.shape["pts"]))
    return jax.shard_map(
        partial(shards, axes),
        mesh=mesh,
        in_specs=(rows,) * 4 + (P(),) * 10,
        out_specs=rows,
        check_vma=False,
    )
```

```python
from functools import partial
import math

import jax
import jax.numpy as jnp
from jax import lax
from jax.experimental import pallas as pl
from jax.experimental.pallas import tpu as pltpu
from jax.sharding import PartitionSpec as P

HEAD = 64
LEAF = 128
BALL = 512
CMP = 256
PAIR = 2 * HEAD
HIDE = 512
CHUNK = 256
MIB = 1 << 20
LATER = 40 * MIB
F32 = jnp.float32
BF16 = jnp.bfloat16
SCALE = HEAD ** (-0.5) * math.log2(math.e)

ANY = pl.BlockSpec(memory_space=pl.ANY)
VMEM = pl.BlockSpec(memory_space=pltpu.VMEM)
SMEM = pl.BlockSpec(memory_space=pltpu.SMEM)


def norm(values, gain):
    wide = values.astype(F32)
    return wide * lax.rsqrt(jnp.mean(wide * wide, axis=-1, keepdims=True) + 1e-06) * gain


def gelu(x):
    c = math.sqrt(2.0 / math.pi)
    t = jnp.tanh(x * (c + (c * 0.044715) * (x * x)))
    return x * (0.5 + 0.5 * t)


def dot(a, b):
    return jnp.dot(a, b, preferred_element_type=F32)


def dot_t(a, b):
    return lax.dot_general(a, b, (((1,), (1,)), ((), ())), preferred_element_type=F32)


def aligned(index, size):
    return pl.ds(pl.multiple_of(index * size, size), size)


def only_head(pair, half):
    lane = lax.broadcasted_iota(jnp.int32, pair.shape, 1)
    return jnp.where((lane >= HEAD) == bool(half), pair, jnp.zeros_like(pair))


def pair_scores(queries, keys):
    both = jnp.concatenate([only_head(queries, 0), only_head(queries, 1)], axis=0)
    return dot_t(both, keys)


def lay_values(out, values):
    keys = values.shape[0]
    ones = jnp.ones_like(values)
    for half in range(2):
        rows = slice(half * keys, (half + 1) * keys)
        out[rows, :PAIR] = only_head(values, half)
        out[rows, PAIR:] = only_head(ones, half)


def weigh(scores, laid):
    rows = scores.shape[0] // 2
    parts = []
    for half in range(2):
        own = scores[half * rows : (half + 1) * rows]
        parts.append(jnp.exp2(own - jnp.max(own, axis=1, keepdims=True)).astype(BF16))
    mixed = dot(jnp.concatenate(parts, axis=1), laid)
    return mixed[:, :PAIR] / mixed[:, PAIR:]


def pipelined(items, first, second):
    held = first(items[0])
    for n, item in enumerate(items):
        now = held
        if n + 1 < len(items):
            held = first(items[n + 1])
        second(item, now)


def send_to(me, s, peers):
    return me ^ s if peers & (peers - 1) == 0 else (me + s) % peers


def got_from(me, s, peers):
    return me ^ s if peers & (peers - 1) == 0 else (me + peers - s) % peers


def start_all(copies):
    for copy in copies:
        copy.start()


def wait_all(copies):
    for copy in copies:
        copy.wait()


def layer_one_kernel(peers, cap, slots, late, *refs):
    me_ref, pick_ref, lead, ids, gain1, gain2, gain3, points, w_in, w_out, w_up, w_down = refs[:12]
    refs = refs[12:]
    if late:
        (h_first, pool_first), refs = refs[:2], refs[2:]
    z_out, h_out, pool_out = refs[:3]
    sends, refs = refs[3 : 3 + len(slots)], refs[3 + len(slots) :]
    x_s, win_s, wout_s, wup_s, wdown_s, q_s, k_s, v_s, bias_s, mix_s, y_s, z_s, h_s, sem, send_sem = refs
    first = lead[0]
    ball = (1 - first) if late else first
    rows = aligned(ball, BALL)
    width = x_s.shape[1]
    hidden = wup_s.shape[1]
    pairs = width // PAIR
    copies = [
        pltpu.make_async_copy(points.at[rows, :], x_s, sem.at[0]),
        pltpu.make_async_copy(w_in, win_s, sem.at[1]),
        pltpu.make_async_copy(w_out, wout_s, sem.at[2]),
        pltpu.make_async_copy(w_up, wup_s, sem.at[3]),
        pltpu.make_async_copy(w_down, wdown_s, sem.at[4]),
    ]
    if late:
        copies.append(pltpu.make_async_copy(h_first, h_s.at[aligned(first, BALL), :], sem.at[5]))
    start_all(copies)

    own = ids[pl.ds(ball, 1), :]
    across = jnp.broadcast_to(own, (LEAF, BALL)).astype(F32)
    down = across.T
    for c in range(BALL // LEAF):
        cols = slice(c * LEAF, (c + 1) * LEAF)
        bias_s[:, cols] = jnp.where(down == across[:1, cols], 0.0, -1e30)

    copies[0].wait()
    h1 = norm(x_s[...], gain1[...]).astype(BF16)
    copies[1].wait()
    q_s[...] = (dot(h1, win_s[:, :width]) * SCALE).astype(BF16)
    k_s[...] = dot(h1, win_s[:, width : 2 * width]).astype(BF16)
    values = dot(h1, win_s[:, 2 * width :]).astype(BF16)
    for g in range(pairs):
        lay_values(v_s.at[g], values[:, g * PAIR : (g + 1) * PAIR])

    def scores(item):
        g, c = item
        cols = slice(g * PAIR, (g + 1) * PAIR)
        return pair_scores(q_s[c * CHUNK : (c + 1) * CHUNK, cols], k_s[:, cols])

    def mix(item, got):
        g, c = item
        at = slice(c * CHUNK, (c + 1) * CHUNK)
        bias = bias_s[at, :]
        out = weigh(got + jnp.concatenate([bias, bias], axis=0), v_s[g])
        mix_s[at, g * PAIR : (g + 1) * PAIR] = out.astype(BF16)

    pipelined([(g, c) for g in range(pairs) for c in range(BALL // CHUNK)], scores, mix)

    copies[2].wait()
    y = (x_s[...].astype(F32) + dot(mix_s[...], wout_s[...])).astype(BF16)
    y_s[...] = y
    inner = norm(y, gain2[...]).astype(BF16)
    copies[3].wait()
    copies[4].wait()
    total = y_s[...].astype(F32)
    for c in range(hidden // HIDE):
        cols = slice(c * HIDE, (c + 1) * HIDE)
        up = gelu(dot(inner, wup_s[:, cols])).astype(BF16)
        total = total + dot(up, wdown_s[cols, :])
    z = total.astype(BF16)
    z_s[...] = z
    h3 = norm(z, gain3[...]).astype(BF16)
    h_s[rows, :] = h3
    me = me_ref[0]
    per = BALL // LEAF
    if late:
        copies[5].wait()
    outgoing = []
    for n, (s, send) in enumerate(zip(slots, sends)):
        for c in range(cap):
            block = jnp.minimum(pick_ref[0, send_to(me, s, peers) * cap + c], 2 * per - 1)
            at = pl.ds(c * LEAF, LEAF)
            outgoing.append(
                pltpu.make_async_copy(h_s.at[aligned(block, LEAF), :], send.at[at, :], send_sem.at[n * cap + c])
            )
    outgoing.append(pltpu.make_async_copy(z_s, z_out, sem.at[6]))
    outgoing.append(pltpu.make_async_copy(h_s.at[rows, :], h_out, sem.at[7]))
    start_all(outgoing)
    wide = h3.astype(F32)
    pooled = []
    for c in range(BALL // CMP):
        pooled.append(jnp.sum(wide[c * CMP : (c + 1) * CMP], axis=0, keepdims=True) * CMP ** (-0.5))
    if late:
        pooled = [pool_first[c : c + 1, :] for c in range(BALL // CMP)] + pooled
        row = lax.broadcasted_iota(jnp.int32, pool_out.shape, 0) - me_ref[1] * len(pooled)
        placed = jnp.zeros(pool_out.shape, F32)
        for c, part in enumerate(pooled):
            placed = jnp.where(row == c, part, placed)
        pool_out[...] = placed.astype(BF16)
    else:
        for c, part in enumerate(pooled):
            pool_out[c : c + 1, :] = part
    wait_all(outgoing)


def layer_one(peers, cap, slots, late, rows, me, pick, lead, ids, gains, points, weights, *first):
    width = points.shape[1]
    hidden = weights[2].shape[1]
    half = jax.ShapeDtypeStruct((BALL, width), BF16)
    block = jax.ShapeDtypeStruct((cap * LEAF, width), BF16)
    pool = jax.ShapeDtypeStruct((rows, width), BF16 if late else F32)
    outs = [half, half, pool] + [block] * len(slots)
    out_specs = [ANY, ANY, VMEM] + [ANY] * len(slots)
    args = [me, pick, lead, ids, *gains, points, *weights]
    specs = [SMEM] * 3 + [VMEM] * 4 + [ANY] * 5
    if late:
        specs += [ANY, VMEM]
        args += first
    return pl.pallas_call(
        partial(layer_one_kernel, peers, cap, slots, late),
        out_shape=outs,
        in_specs=specs,
        out_specs=out_specs,
        scratch_shapes=[
            pltpu.VMEM((BALL, width), BF16),
            pltpu.VMEM((width, 3 * width), BF16),
            pltpu.VMEM((width, width), BF16),
            pltpu.VMEM((width, hidden), BF16),
            pltpu.VMEM((hidden, width), BF16),
            pltpu.VMEM((BALL, width), BF16),
            pltpu.VMEM((BALL, width), BF16),
            pltpu.VMEM((width // PAIR, 2 * BALL, 2 * PAIR), BF16),
            pltpu.VMEM((BALL, BALL), F32),
            pltpu.VMEM((BALL, width), BF16),
            pltpu.VMEM((BALL, width), BF16),
            pltpu.VMEM((BALL, width), BF16),
            pltpu.VMEM((points.shape[0], width), BF16),
            pltpu.SemaphoreType.DMA((8,)),
            pltpu.SemaphoreType.DMA((len(slots) * cap,)),
        ],
        compiler_params=pltpu.CompilerParams(vmem_limit_bytes=60 * MIB),
        cost_estimate=pl.CostEstimate(
            flops=2 * BALL * width * (4 * width + 2 * hidden) + 16 * BALL * BALL * width,
            bytes_accessed=8 * MIB,
            transcendentals=BALL * BALL * width // HEAD,
        ),
        name="layer_one_late" if late else "layer_one_lead",
    )(*args)


def place_of(recv_ref, slot, blocks):
    place, found = jnp.int32(0), jnp.int32(0)
    for j in range(blocks):
        hit = (recv_ref[0, j] == slot).astype(jnp.int32)
        place = place + j * hit
        found = found + hit
    return place, found > 0


def layer_two_kernel(peers, cap, blocks, start, columns, *refs):
    me_ref, recv_ref = refs[:2]
    arrived = refs[2 : 2 + peers]
    w_in = refs[2 + peers]
    outs = refs[3 + peers : 3 + 2 * peers]
    h_s, w_s, q_s, k_s, v_s, a_s, sem, block_sem = refs[3 + 2 * peers :]
    width = h_s.shape[1]
    pairs = columns // PAIR
    me = me_ref[0]
    balls = blocks * LEAF // BALL
    copies = []
    for i in range(3):
        cols = pl.ds(i * width + start, columns)
        copies.append(
            pltpu.make_async_copy(w_in.at[:, cols], w_s.at[:, pl.ds(i * columns, columns)], sem.at[i])
        )
    start_all(copies)
    places, moves = [], []
    for s in range(peers):
        for c in range(cap):
            place, found = place_of(recv_ref, got_from(me, s, peers) * cap + c, blocks)
            at = pl.ds(c * LEAF, LEAF)
            move = pltpu.make_async_copy(
                arrived[s].at[at, :], h_s.at[aligned(place, LEAF), :], block_sem.at[s * cap + c]
            )
            places.append(place)
            moves.append((found, move))
            pl.when(found)(move.start)
    wait_all(copies)
    for found, move in moves:
        pl.when(found)(move.wait)
    for b in range(balls):
        rows = slice(b * BALL, (b + 1) * BALL)
        h = h_s[rows, :]
        q_s[rows, :] = (dot(h, w_s[:, :columns]) * SCALE).astype(BF16)
        k_s[rows, :] = dot(h, w_s[:, columns : 2 * columns]).astype(BF16)
        values = dot(h, w_s[:, 2 * columns :]).astype(BF16)
        for g in range(pairs):
            lay_values(v_s.at[b * pairs + g], values[:, g * PAIR : (g + 1) * PAIR])

    def scores(item):
        b, g, c = item
        cols = slice(g * PAIR, (g + 1) * PAIR)
        at = b * BALL + c * CHUNK
        return pair_scores(q_s[at : at + CHUNK, cols], k_s[b * BALL : (b + 1) * BALL, cols])

    def mix(item, got):
        b, g, c = item
        at = b * BALL + c * CHUNK
        a_s[at : at + CHUNK, g * PAIR : (g + 1) * PAIR] = weigh(got, v_s[b * pairs + g]).astype(BF16)

    pipelined(
        [(b, g, c) for b in range(balls) for g in range(pairs) for c in range(BALL // CHUNK)], scores, mix
    )
    outgoing = []
    for s in range(peers):
        for c in range(cap):
            n = s * cap + c
            at = pl.ds(c * LEAF, LEAF)
            outgoing.append(
                pltpu.make_async_copy(a_s.at[aligned(places[n], LEAF), :], outs[s].at[at, :], block_sem.at[n])
            )
    start_all(outgoing)
    wait_all(outgoing)


def layer_two(peers, cap, start, columns, me, recv, arrived, w_in):
    blocks = recv.shape[1]
    width = w_in.shape[0]
    pairs = columns // PAIR
    rows = blocks * LEAF
    block = jax.ShapeDtypeStruct((cap * LEAF, columns), BF16)
    return pl.pallas_call(
        partial(layer_two_kernel, peers, cap, blocks, start, columns),
        out_shape=[block] * peers,
        in_specs=[SMEM, SMEM] + [ANY] * (peers + 1),
        out_specs=[ANY] * peers,
        scratch_shapes=[
            pltpu.VMEM((rows, width), BF16),
            pltpu.VMEM((width, 3 * columns), BF16),
            pltpu.VMEM((rows, columns), BF16),
            pltpu.VMEM((rows, columns), BF16),
            pltpu.VMEM((rows // BALL * pairs, 2 * BALL, 2 * PAIR), BF16),
            pltpu.VMEM((rows, columns), BF16),
            pltpu.SemaphoreType.DMA((3,)),
            pltpu.SemaphoreType.DMA((peers * cap,)),
        ],
        compiler_params=pltpu.CompilerParams(vmem_limit_bytes=LATER),
        cost_estimate=pl.CostEstimate(
            flops=rows * columns * (6 * width + 16 * BALL),
            bytes_accessed=4 * MIB,
            transcendentals=rows * BALL * columns // HEAD,
        ),
        name=f"layer_two_{start}",
    )(me, recv, *arrived, w_in)


def compressed_kernel(*refs):
    lead, h_first, h_late, z_first, z_late, pooled, w_comp, w_in, w_out, out = refs[:10]
    h_s, z_s, p_s, wc_s, wq_s, wo_s, q_s, ck_s, cv_s, a_s, o_s, sem, out_sem = refs[10:]
    rows, width = h_s.shape
    pairs = width // PAIR
    first = lead[0]
    copies = [
        pltpu.make_async_copy(pooled, p_s, sem.at[0]),
        pltpu.make_async_copy(w_comp, wc_s, sem.at[1]),
        pltpu.make_async_copy(w_in.at[:, pl.ds(0, width)], wq_s, sem.at[2]),
        pltpu.make_async_copy(h_first, h_s.at[aligned(first, BALL), :], sem.at[3]),
        pltpu.make_async_copy(h_late, h_s.at[aligned(1 - first, BALL), :], sem.at[4]),
        pltpu.make_async_copy(w_out, wo_s, sem.at[5]),
        pltpu.make_async_copy(z_first, z_s.at[aligned(first, BALL), :], sem.at[6]),
        pltpu.make_async_copy(z_late, z_s.at[aligned(1 - first, BALL), :], sem.at[7]),
    ]
    start_all(copies)
    wait_all(copies[:2])
    far = dot(p_s[...], wc_s[...]).astype(BF16)
    ck_s[...] = far[:, :width]
    for g in range(pairs):
        lay_values(cv_s.at[g], far[:, width + g * PAIR : width + (g + 1) * PAIR])
    wait_all(copies[2:5])
    q_s[...] = (dot(h_s[...], wq_s[...]) * SCALE).astype(BF16)

    def scores(item):
        g, c = item
        cols = slice(g * PAIR, (g + 1) * PAIR)
        return pair_scores(q_s[c * CHUNK : (c + 1) * CHUNK, cols], ck_s[:, cols])

    def mix(item, got):
        g, c = item
        a_s[c * CHUNK : (c + 1) * CHUNK, g * PAIR : (g + 1) * PAIR] = weigh(got, cv_s[g]).astype(BF16)

    pipelined([(g, c) for c in range(rows // CHUNK) for g in range(pairs)], scores, mix)
    wait_all(copies[5:])
    outgoing = []
    for c in range(rows // CHUNK):
        at = slice(c * CHUNK, (c + 1) * CHUNK)
        o_s[at, :] = z_s[at, :].astype(F32) + dot(a_s[at, :], wo_s[...])
        there = pl.ds(c * CHUNK, CHUNK)
        copy = pltpu.make_async_copy(o_s.at[there, :], out.at[there, :], out_sem.at[c])
        copy.start()
        outgoing.append(copy)
    wait_all(outgoing)


def compressed(lead, h_first, h_late, z_first, z_late, pooled, w_comp, w_in, w_out):
    rows, width = 2 * h_first.shape[0], h_first.shape[1]
    comp = pooled.shape[0]
    return pl.pallas_call(
        compressed_kernel,
        out_shape=jax.ShapeDtypeStruct((rows, width), F32),
        in_specs=[SMEM] + [ANY] * 8,
        out_specs=ANY,
        scratch_shapes=[
            pltpu.VMEM((rows, width), BF16),
            pltpu.VMEM((rows, width), BF16),
            pltpu.VMEM((comp, width), BF16),
            pltpu.VMEM((width, 2 * width), BF16),
            pltpu.VMEM((width, width), BF16),
            pltpu.VMEM((width, width), BF16),
            pltpu.VMEM((rows, width), BF16),
            pltpu.VMEM((comp, width), BF16),
            pltpu.VMEM((width // PAIR, 2 * comp, 2 * PAIR), BF16),
            pltpu.VMEM((rows, width), BF16),
            pltpu.VMEM((rows, width), F32),
            pltpu.SemaphoreType.DMA((8,)),
            pltpu.SemaphoreType.DMA((rows // CHUNK,)),
        ],
        compiler_params=pltpu.CompilerParams(vmem_limit_bytes=60 * MIB),
        cost_estimate=pl.CostEstimate(
            flops=rows * width * (4 * width + 16 * comp),
            bytes_accessed=8 * MIB,
            transcendentals=rows * comp * width // HEAD,
        ),
        name="compressed",
    )(lead, h_first, h_late, z_first, z_late, pooled, w_comp, w_in, w_out)


def final_kernel(peers, cap, bounds, me_ref, pick_ref, *refs):
    parts = len(bounds)
    back = [refs[p * peers : (p + 1) * peers] for p in range(parts)]
    w_out, base, out, w_s, b_s, m_s, o_s, sem, block_sem, out_sem = refs[parts * peers :]
    blocks = b_s.shape[0] // LEAF
    me = me_ref[0]
    copies = [
        pltpu.make_async_copy(w_out, w_s, sem.at[0]),
        pltpu.make_async_copy(base, b_s, sem.at[1]),
    ]
    start_all(copies)
    moves = []
    for p, (start, columns) in enumerate(bounds):
        for s in range(peers):
            for c in range(cap):
                block = pick_ref[0, send_to(me, s, peers) * cap + c]
                found = block < blocks
                at = pl.ds(c * LEAF, LEAF)
                place = aligned(jnp.minimum(block, blocks - 1), LEAF)
                move = pltpu.make_async_copy(
                    back[p][s].at[at, :],
                    m_s.at[place, pl.ds(start, columns)],
                    block_sem.at[(p * peers + s) * cap + c],
                )
                moves.append((found, move))
                pl.when(found)(move.start)
    wait_all(copies)
    for found, move in moves:
        pl.when(found)(move.wait)
    outgoing = []
    for b in range(b_s.shape[0] // CHUNK):
        rows = slice(b * CHUNK, (b + 1) * CHUNK)
        o_s[rows, :] = (b_s[rows, :] + dot(m_s[rows, :], w_s[...])).astype(BF16)
        at = pl.ds(b * CHUNK, CHUNK)
        copy = pltpu.make_async_copy(o_s.at[at, :], out.at[at, :], out_sem.at[b])
        copy.start()
        outgoing.append(copy)
    wait_all(outgoing)


def final(peers, cap, bounds, me, pick, back, w_out, base):
    rows, width = base.shape
    return pl.pallas_call(
        partial(final_kernel, peers, cap, bounds),
        out_shape=jax.ShapeDtypeStruct((rows, width), BF16),
        in_specs=[SMEM] * 2 + [ANY] * (peers * len(bounds) + 2),
        out_specs=ANY,
        scratch_shapes=[
            pltpu.VMEM((width, width), BF16),
            pltpu.VMEM((rows, width), F32),
            pltpu.VMEM((rows, width), BF16),
            pltpu.VMEM((rows, width), BF16),
            pltpu.SemaphoreType.DMA((2,)),
            pltpu.SemaphoreType.DMA((len(bounds) * peers * cap,)),
            pltpu.SemaphoreType.DMA((rows // CHUNK,)),
        ],
        compiler_params=pltpu.CompilerParams(vmem_limit_bytes=LATER),
        cost_estimate=pl.CostEstimate(
            flops=2 * rows * width * width, bytes_accessed=4 * MIB, transcendentals=0
        ),
        name="last_product",
    )(me, pick, *back, w_out, base)


def shards(
    axes,
    points,
    ball_ids,
    send_pick,
    recv_from,
    gain_one,
    attn_in_one,
    attn_out_one,
    gain_two,
    mlp_up,
    mlp_down,
    gain_three,
    compress_proj,
    attn_in_two,
    attn_out_two,
):
    peers = axes[1][1]
    cap = send_pick.shape[1] // peers
    per = BALL // LEAF
    width = points.shape[1]
    me = lax.axis_index("pts").astype(jnp.int32)
    far = peers - 1
    target = send_to(me, far, peers)
    lead_slot = lax.dynamic_slice(send_pick[0], (target * cap,), (1,))
    lead = jnp.minimum(lead_slot // per, ball_ids.shape[0] - 1).astype(jnp.int32)
    place = lax.axis_index("grp").astype(jnp.int32) * peers + me
    me1 = jnp.stack([me, place])
    gains = tuple(g.reshape(1, -1) for g in (gain_one, gain_two, gain_three))
    weights = (attn_in_one, attn_out_one, mlp_up, mlp_down)
    one = partial(layer_one, peers, cap)

    def travel(blocks, s, home):
        if s == 0:
            return blocks
        pattern = [(i, send_to(i, s, peers)) for i in range(peers)]
        if home:
            pattern = [(b, a) for a, b in pattern]
        return lax.ppermute(blocks, "pts", pattern)

    early = [far] if cap == 1 else []
    local = points.shape[0] // CMP
    z_first, h_first, pool_first, *lead_sends = one(
        early, False, local // 2, me1, send_pick, lead, ball_ids, gains, points, weights
    )
    arrived = {s: travel(b, s, False) for s, b in zip(early, lead_sends)}
    order = [s for s in range(peers) if s not in early]
    every = local * axes[0][1] * peers
    late_outs = one(
        order, True, every, me1, send_pick, lead, ball_ids, gains, points, weights, h_first, pool_first
    )
    late_outs, arrived = lax.optimization_barrier((late_outs, arrived))
    z_late, h_late, placed, *late_sends = late_outs
    arrived.update({s: travel(b, s, False) for s, b in zip(order, late_sends)})
    pooled = lax.psum(placed, ("grp", "pts"))
    bounds = [(0, width // 2), (width // 2, width // 2)]
    back = []
    for start, columns in bounds:
        mixed = layer_two(
            peers, cap, start, columns, me1, recv_from, [arrived[s] for s in range(peers)], attn_in_two
        )
        part = {s: travel(mixed[s], s, True) for s in range(peers)}
        back.extend(part[s] for s in range(peers))
    base = compressed(
        lead, h_first, h_late, z_first, z_late, pooled, compress_proj, attn_in_two, attn_out_two
    )
    return final(peers, cap, bounds, me1, send_pick, back, attn_out_two, base)


def solution(mesh):
    rows = P(("grp", "pts"), None)
    axes = (("grp", mesh.shape["grp"]), ("pts", mesh.shape["pts"]))
    return jax.shard_map(
        partial(shards, axes),
        mesh=mesh,
        in_specs=(rows,) * 4 + (P(),) * 10,
        out_specs=rows,
        check_vma=False,
    )
```

```python
from functools import partial
import math

import jax
import jax.numpy as jnp
from jax import lax
from jax.experimental import pallas as pl
from jax.experimental.pallas import tpu as pltpu
from jax.sharding import PartitionSpec as P

HEAD = 64
LEAF = 128
BALL = 512
CMP = 256
PAIR = 2 * HEAD
HIDE = 512
CHUNK = 256
MIB = 1 << 20
LATER = 40 * MIB
F32 = jnp.float32
BF16 = jnp.bfloat16
SCALE = HEAD ** (-0.5) * math.log2(math.e)

ANY = pl.BlockSpec(memory_space=pl.ANY)
VMEM = pl.BlockSpec(memory_space=pltpu.VMEM)
SMEM = pl.BlockSpec(memory_space=pltpu.SMEM)


def norm(values, gain):
    wide = values.astype(F32)
    return wide * lax.rsqrt(jnp.mean(wide * wide, axis=-1, keepdims=True) + 1e-06) * gain


def gelu(x):
    c = math.sqrt(2.0 / math.pi)
    t = jnp.tanh(x * (c + (c * 0.044715) * (x * x)))
    return x * (0.5 + 0.5 * t)


def dot(a, b):
    return jnp.dot(a, b, preferred_element_type=F32)


def dot_t(a, b):
    return lax.dot_general(a, b, (((1,), (1,)), ((), ())), preferred_element_type=F32)


def aligned(index, size):
    return pl.ds(pl.multiple_of(index * size, size), size)


def only_head(pair, half):
    lane = lax.broadcasted_iota(jnp.int32, pair.shape, 1)
    return jnp.where((lane >= HEAD) == bool(half), pair, jnp.zeros_like(pair))


def pair_scores(queries, keys):
    both = jnp.concatenate([only_head(queries, 0), only_head(queries, 1)], axis=0)
    return dot_t(both, keys)


def lay_values(out, values):
    keys = values.shape[0]
    ones = jnp.ones_like(values)
    for half in range(2):
        rows = slice(half * keys, (half + 1) * keys)
        out[rows, :PAIR] = only_head(values, half)
        out[rows, PAIR:] = only_head(ones, half)


def weigh(scores, laid):
    rows = scores.shape[0] // 2
    parts = []
    for half in range(2):
        own = scores[half * rows : (half + 1) * rows]
        parts.append(jnp.exp2(own - jnp.max(own, axis=1, keepdims=True)).astype(BF16))
    mixed = dot(jnp.concatenate(parts, axis=1), laid)
    return mixed[:, :PAIR] / mixed[:, PAIR:]


def pipelined(items, first, second):
    held = first(items[0])
    for n, item in enumerate(items):
        now = held
        if n + 1 < len(items):
            held = first(items[n + 1])
        second(item, now)


def send_to(me, s, peers):
    return me ^ s if peers & (peers - 1) == 0 else (me + s) % peers


def got_from(me, s, peers):
    return me ^ s if peers & (peers - 1) == 0 else (me + peers - s) % peers


def start_all(copies):
    for copy in copies:
        copy.start()


def wait_all(copies):
    for copy in copies:
        copy.wait()


def feed_forward(y, gain2, gain3, up_s, down_s):
    inner = norm(y, gain2[...]).astype(BF16)
    total = y.astype(F32)
    for c in range(up_s.shape[1] // HIDE):
        cols = slice(c * HIDE, (c + 1) * HIDE)
        up = gelu(dot(inner, up_s[:, cols])).astype(BF16)
        total = total + dot(up, down_s[cols, :])
    z = total.astype(BF16)
    return z, norm(z, gain3[...]).astype(BF16)


def layer_one_kernel(peers, cap, *refs):
    pick_ref, ids, gain1, gain2, gain3, points, w_in, w_out, w_up, w_down = refs[:10]
    z_out, h_out, pool_out = refs[10:13]
    sends, refs = refs[13 : 13 + peers], refs[13 + peers :]
    x_s, in_s, wo_s, up_s, down_s, q_s, k_s, v_s, bias_s, mix_s, y_s, z_s, h_s, sem, send_sem = refs
    me = lax.axis_index("pts").astype(jnp.int32)
    count, width = x_s.shape
    balls = count // BALL
    pairs = width // PAIR
    blocks = count // LEAF
    copies = [
        pltpu.make_async_copy(points, x_s, sem.at[0]),
        pltpu.make_async_copy(w_in, in_s, sem.at[1]),
        pltpu.make_async_copy(w_out, wo_s, sem.at[2]),
        pltpu.make_async_copy(w_up, up_s, sem.at[3]),
        pltpu.make_async_copy(w_down, down_s, sem.at[4]),
    ]
    start_all(copies)
    for b in range(balls):
        across = jnp.broadcast_to(ids[b : b + 1, :], (LEAF, BALL)).astype(F32)
        down = across.T
        for c in range(BALL // LEAF):
            cols = slice(c * LEAF, (c + 1) * LEAF)
            bias_s[b, :, cols] = jnp.where(down == across[:1, cols], 0.0, -1e30)
    copies[0].wait()
    for b in range(balls):
        rows = slice(b * BALL, (b + 1) * BALL)
        h1 = norm(x_s[rows, :], gain1[...]).astype(BF16)
        if b == 0:
            copies[1].wait()
        q_s[rows, :] = (dot(h1, in_s[:, :width]) * SCALE).astype(BF16)
        k_s[rows, :] = dot(h1, in_s[:, width : 2 * width]).astype(BF16)
        values = dot(h1, in_s[:, 2 * width :]).astype(BF16)
        for g in range(pairs):
            lay_values(v_s.at[b * pairs + g], values[:, g * PAIR : (g + 1) * PAIR])

    def scores(item):
        b, g, c = item
        cols = slice(g * PAIR, (g + 1) * PAIR)
        at = b * BALL + c * CHUNK
        return pair_scores(q_s[at : at + CHUNK, cols], k_s[b * BALL : (b + 1) * BALL, cols])

    def mix(item, got):
        b, g, c = item
        at = b * BALL + c * CHUNK
        bias = bias_s[b, c * CHUNK : (c + 1) * CHUNK, :]
        out = weigh(got + jnp.concatenate([bias, bias], axis=0), v_s[b * pairs + g])
        mix_s[at : at + CHUNK, g * PAIR : (g + 1) * PAIR] = out.astype(BF16)

    pipelined(
        [(b, g, c) for b in range(balls) for g in range(pairs) for c in range(BALL // CHUNK)], scores, mix
    )
    copies[2].wait()
    for b in range(balls):
        rows = slice(b * BALL, (b + 1) * BALL)
        y_s[rows, :] = (x_s[rows, :].astype(F32) + dot(mix_s[rows, :], wo_s[...])).astype(BF16)
    copies[3].wait()
    copies[4].wait()
    outgoing = []
    for b in range(balls):
        rows = slice(b * BALL, (b + 1) * BALL)
        z, h3 = feed_forward(y_s[rows, :], gain2, gain3, up_s, down_s)
        z_s[rows, :] = z
        h_s[rows, :] = h3
        wide = h3.astype(F32)
        for c in range(BALL // CMP):
            part = jnp.sum(wide[c * CMP : (c + 1) * CMP], axis=0, keepdims=True) * CMP ** (-0.5)
            at = b * (BALL // CMP) + c
            pool_out[at : at + 1, :] = part.astype(BF16)
        at = pl.ds(b * BALL, BALL)
        for n, (source, there) in enumerate(((z_s, z_out), (h_s, h_out))):
            copy = pltpu.make_async_copy(source.at[at, :], there.at[at, :], sem.at[5 + 2 * b + n])
            copy.start()
            outgoing.append(copy)
    for s in range(peers - 1, -1, -1):
        for c in range(cap):
            slot = send_to(me, s, peers) * cap + c
            block = jnp.minimum(pick_ref[0, slot], blocks - 1)
            there = sends[s].at[pl.ds(c * LEAF, LEAF), :]
            copy = pltpu.make_async_copy(h_s.at[aligned(block, LEAF), :], there, send_sem.at[s * cap + c])
            copy.start()
            outgoing.append(copy)
    wait_all(outgoing)


def layer_one(peers, cap, pick, ids, gains, points, weights):
    count, width = points.shape
    hidden = weights[2].shape[1]
    whole = jax.ShapeDtypeStruct((count, width), BF16)
    block = jax.ShapeDtypeStruct((cap * LEAF, width), BF16)
    pool = jax.ShapeDtypeStruct((count // CMP, width), BF16)
    balls = count // BALL
    return pl.pallas_call(
        partial(layer_one_kernel, peers, cap),
        out_shape=[whole, whole, pool] + [block] * peers,
        in_specs=[SMEM] + [VMEM] * 4 + [ANY] * 5,
        out_specs=[ANY, ANY, VMEM] + [ANY] * peers,
        scratch_shapes=[
            pltpu.VMEM((count, width), BF16),
            pltpu.VMEM((width, 3 * width), BF16),
            pltpu.VMEM((width, width), BF16),
            pltpu.VMEM((width, hidden), BF16),
            pltpu.VMEM((hidden, width), BF16),
            pltpu.VMEM((count, width), BF16),
            pltpu.VMEM((count, width), BF16),
            pltpu.VMEM((balls * width // PAIR, 2 * BALL, 2 * PAIR), BF16),
            pltpu.VMEM((balls, BALL, BALL), F32),
            pltpu.VMEM((count, width), BF16),
            pltpu.VMEM((count, width), BF16),
            pltpu.VMEM((count, width), BF16),
            pltpu.VMEM((count, width), BF16),
            pltpu.SemaphoreType.DMA((5 + 2 * balls,)),
            pltpu.SemaphoreType.DMA((peers * cap,)),
        ],
        compiler_params=pltpu.CompilerParams(vmem_limit_bytes=60 * MIB),
        cost_estimate=pl.CostEstimate(
            flops=count * width * (8 * width + 4 * hidden + 16 * BALL),
            bytes_accessed=10 * MIB,
            transcendentals=count * BALL * width // HEAD,
        ),
        name="layer_one",
    )(pick, ids, *gains, points, *weights)


def place_of(recv_ref, slot, blocks):
    place, found = jnp.int32(0), jnp.int32(0)
    for j in range(blocks):
        hit = (recv_ref[0, j] == slot).astype(jnp.int32)
        place = place + j * hit
        found = found + hit
    return place, found > 0


def layer_two_kernel(peers, cap, blocks, start, columns, *refs):
    recv_ref = refs[0]
    arrived = refs[1 : 1 + peers][::-1]
    w_in = refs[1 + peers]
    outs = refs[2 + peers : 2 + 2 * peers]
    h_s, w_s, q_s, k_s, v_s, a_s, sem, block_sem = refs[2 + 2 * peers :]
    width = h_s.shape[1]
    pairs = columns // PAIR
    me = lax.axis_index("pts").astype(jnp.int32)
    balls = blocks * LEAF // BALL
    copies = []
    for i in range(3):
        cols = pl.ds(i * width + start, columns)
        copies.append(
            pltpu.make_async_copy(w_in.at[:, cols], w_s.at[:, pl.ds(i * columns, columns)], sem.at[i])
        )
    start_all(copies)
    places, moves = [], []
    for s in range(peers):
        for c in range(cap):
            place, found = place_of(recv_ref, got_from(me, s, peers) * cap + c, blocks)
            at = pl.ds(c * LEAF, LEAF)
            move = pltpu.make_async_copy(
                arrived[s].at[at, :], h_s.at[aligned(place, LEAF), :], block_sem.at[s * cap + c]
            )
            places.append(place)
            moves.append((found, move))
            pl.when(found)(move.start)
    wait_all(copies)
    for found, move in moves:
        pl.when(found)(move.wait)
    for b in range(balls):
        rows = slice(b * BALL, (b + 1) * BALL)
        h = h_s[rows, :]
        q_s[rows, :] = (dot(h, w_s[:, :columns]) * SCALE).astype(BF16)
        k_s[rows, :] = dot(h, w_s[:, columns : 2 * columns]).astype(BF16)
        values = dot(h, w_s[:, 2 * columns :]).astype(BF16)
        for g in range(pairs):
            lay_values(v_s.at[b * pairs + g], values[:, g * PAIR : (g + 1) * PAIR])

    def scores(item):
        b, g, c = item
        cols = slice(g * PAIR, (g + 1) * PAIR)
        at = b * BALL + c * CHUNK
        return pair_scores(q_s[at : at + CHUNK, cols], k_s[b * BALL : (b + 1) * BALL, cols])

    def mix(item, got):
        b, g, c = item
        at = b * BALL + c * CHUNK
        a_s[at : at + CHUNK, g * PAIR : (g + 1) * PAIR] = weigh(got, v_s[b * pairs + g]).astype(BF16)

    pipelined(
        [(b, g, c) for b in range(balls) for g in range(pairs) for c in range(BALL // CHUNK)], scores, mix
    )
    outgoing = []
    for s in range(peers):
        for c in range(cap):
            n = s * cap + c
            at = pl.ds(c * LEAF, LEAF)
            outgoing.append(
                pltpu.make_async_copy(a_s.at[aligned(places[n], LEAF), :], outs[s].at[at, :], block_sem.at[n])
            )
    start_all(outgoing)
    wait_all(outgoing)


def layer_two(peers, cap, start, columns, recv, arrived, w_in):
    blocks = recv.shape[1]
    width = w_in.shape[0]
    pairs = columns // PAIR
    rows = blocks * LEAF
    block = jax.ShapeDtypeStruct((cap * LEAF, columns), BF16)
    return pl.pallas_call(
        partial(layer_two_kernel, peers, cap, blocks, start, columns),
        out_shape=[block] * peers,
        in_specs=[SMEM] + [ANY] * (peers + 1),
        out_specs=[ANY] * peers,
        scratch_shapes=[
            pltpu.VMEM((rows, width), BF16),
            pltpu.VMEM((width, 3 * columns), BF16),
            pltpu.VMEM((rows, columns), BF16),
            pltpu.VMEM((rows, columns), BF16),
            pltpu.VMEM((rows // BALL * pairs, 2 * BALL, 2 * PAIR), BF16),
            pltpu.VMEM((rows, columns), BF16),
            pltpu.SemaphoreType.DMA((3,)),
            pltpu.SemaphoreType.DMA((peers * cap,)),
        ],
        compiler_params=pltpu.CompilerParams(vmem_limit_bytes=LATER),
        cost_estimate=pl.CostEstimate(
            flops=rows * columns * (6 * width + 16 * BALL),
            bytes_accessed=4 * MIB,
            transcendentals=rows * BALL * columns // HEAD,
        ),
        name=f"layer_two_{start}",
    )(recv, *arrived[::-1], w_in)


def compressed_kernel(h, z, pool_a, pool_b, w_comp, w_in, w_out, out, *scratch):
    h_s, z_s, p_s, wc_s, wq_s, wo_s, q_s, ck_s, cv_s, a_s, o_s, sem, out_sem = scratch
    rows, width = h_s.shape
    pairs = width // PAIR
    near = pool_a.shape[0]
    copies = [
        pltpu.make_async_copy(pool_a, p_s.at[pl.ds(0, near), :], sem.at[0]),
        pltpu.make_async_copy(pool_b, p_s.at[pl.ds(near, pool_b.shape[0]), :], sem.at[1]),
        pltpu.make_async_copy(w_comp, wc_s, sem.at[2]),
        pltpu.make_async_copy(w_in.at[:, pl.ds(0, width)], wq_s, sem.at[3]),
        pltpu.make_async_copy(h, h_s, sem.at[4]),
        pltpu.make_async_copy(w_out, wo_s, sem.at[5]),
        pltpu.make_async_copy(z, z_s, sem.at[6]),
    ]
    start_all(copies)
    wait_all(copies[:3])
    far = dot(p_s[...], wc_s[...]).astype(BF16)
    ck_s[...] = far[:, :width]
    for g in range(pairs):
        lay_values(cv_s.at[g], far[:, width + g * PAIR : width + (g + 1) * PAIR])
    wait_all(copies[3:5])
    q_s[...] = (dot(h_s[...], wq_s[...]) * SCALE).astype(BF16)

    def scores(item):
        g, c = item
        cols = slice(g * PAIR, (g + 1) * PAIR)
        return pair_scores(q_s[c * CHUNK : (c + 1) * CHUNK, cols], ck_s[:, cols])

    def mix(item, got):
        g, c = item
        a_s[c * CHUNK : (c + 1) * CHUNK, g * PAIR : (g + 1) * PAIR] = weigh(got, cv_s[g]).astype(BF16)

    pipelined([(g, c) for c in range(rows // CHUNK) for g in range(pairs)], scores, mix)
    wait_all(copies[5:])
    outgoing = []
    for c in range(rows // CHUNK):
        at = slice(c * CHUNK, (c + 1) * CHUNK)
        o_s[at, :] = z_s[at, :].astype(F32) + dot(a_s[at, :], wo_s[...])
        there = pl.ds(c * CHUNK, CHUNK)
        copy = pltpu.make_async_copy(o_s.at[there, :], out.at[there, :], out_sem.at[c])
        copy.start()
        outgoing.append(copy)
    wait_all(outgoing)


def compressed(h, z, pooled, w_comp, w_in, w_out):
    rows, width = h.shape
    comp = sum(p.shape[0] for p in pooled)
    return pl.pallas_call(
        compressed_kernel,
        out_shape=jax.ShapeDtypeStruct((rows, width), F32),
        in_specs=[ANY] * 7,
        out_specs=ANY,
        scratch_shapes=[
            pltpu.VMEM((rows, width), BF16),
            pltpu.VMEM((rows, width), BF16),
            pltpu.VMEM((comp, width), BF16),
            pltpu.VMEM((width, 2 * width), BF16),
            pltpu.VMEM((width, width), BF16),
            pltpu.VMEM((width, width), BF16),
            pltpu.VMEM((rows, width), BF16),
            pltpu.VMEM((comp, width), BF16),
            pltpu.VMEM((width // PAIR, 2 * comp, 2 * PAIR), BF16),
            pltpu.VMEM((rows, width), BF16),
            pltpu.VMEM((rows, width), F32),
            pltpu.SemaphoreType.DMA((7,)),
            pltpu.SemaphoreType.DMA((rows // CHUNK,)),
        ],
        compiler_params=pltpu.CompilerParams(vmem_limit_bytes=60 * MIB),
        cost_estimate=pl.CostEstimate(
            flops=rows * width * (4 * width + 16 * comp),
            bytes_accessed=8 * MIB,
            transcendentals=rows * comp * width // HEAD,
        ),
        name="compressed",
    )(h, z, *pooled, w_comp, w_in, w_out)


def final_kernel(peers, cap, bounds, pick_ref, *refs):
    parts = len(bounds)
    back = [refs[p * peers : (p + 1) * peers][::-1] for p in range(parts)]
    w_out, base, out, w_s, b_s, m_s, o_s, sem, block_sem, out_sem = refs[parts * peers :]
    blocks = b_s.shape[0] // LEAF
    me = lax.axis_index("pts").astype(jnp.int32)
    copies = [
        pltpu.make_async_copy(w_out, w_s, sem.at[0]),
        pltpu.make_async_copy(base, b_s, sem.at[1]),
    ]
    start_all(copies)
    moves = []
    for p, (start, columns) in enumerate(bounds):
        for s in range(peers):
            for c in range(cap):
                block = pick_ref[0, send_to(me, s, peers) * cap + c]
                found = block < blocks
                at = pl.ds(c * LEAF, LEAF)
                place = aligned(jnp.minimum(block, blocks - 1), LEAF)
                move = pltpu.make_async_copy(
                    back[p][s].at[at, :],
                    m_s.at[place, pl.ds(start, columns)],
                    block_sem.at[(p * peers + s) * cap + c],
                )
                moves.append((found, move))
                pl.when(found)(move.start)
    wait_all(copies)
    for found, move in moves:
        pl.when(found)(move.wait)
    outgoing = []
    for b in range(b_s.shape[0] // CHUNK):
        rows = slice(b * CHUNK, (b + 1) * CHUNK)
        o_s[rows, :] = (b_s[rows, :] + dot(m_s[rows, :], w_s[...])).astype(BF16)
        at = pl.ds(b * CHUNK, CHUNK)
        copy = pltpu.make_async_copy(o_s.at[at, :], out.at[at, :], out_sem.at[b])
        copy.start()
        outgoing.append(copy)
    wait_all(outgoing)


def final(peers, cap, bounds, pick, back, w_out, base):
    rows, width = base.shape
    return pl.pallas_call(
        partial(final_kernel, peers, cap, bounds),
        out_shape=jax.ShapeDtypeStruct((rows, width), BF16),
        in_specs=[SMEM] + [ANY] * (peers * len(bounds) + 2),
        out_specs=ANY,
        scratch_shapes=[
            pltpu.VMEM((width, width), BF16),
            pltpu.VMEM((rows, width), F32),
            pltpu.VMEM((rows, width), BF16),
            pltpu.VMEM((rows, width), BF16),
            pltpu.SemaphoreType.DMA((2,)),
            pltpu.SemaphoreType.DMA((len(bounds) * peers * cap,)),
            pltpu.SemaphoreType.DMA((rows // CHUNK,)),
        ],
        compiler_params=pltpu.CompilerParams(vmem_limit_bytes=LATER),
        cost_estimate=pl.CostEstimate(
            flops=2 * rows * width * width, bytes_accessed=4 * MIB, transcendentals=0
        ),
        name="last_product",
    )(pick, *back, w_out, base)


def xor_pairs(size, s):
    return [(i, i ^ s) for i in range(size)]


def gather_all(rows, axes):
    (grp, groups), (pts, peers) = axes
    if groups & (groups - 1) or peers & (peers - 1) or peers == 1:
        rows = lax.all_gather(rows, (grp, pts), axis=0, tiled=True)
        return rows[: rows.shape[0] // 2], rows[rows.shape[0] // 2 :]
    for axis, shifts in ((grp, range(1, groups)), (pts, range(2, peers, 2))):
        pieces = [rows] + [lax.ppermute(rows, axis, xor_pairs(axes[axis == pts][1], s)) for s in shifts]
        rows = lax.optimization_barrier(jnp.concatenate(pieces))
    return rows, lax.ppermute(rows, pts, xor_pairs(peers, 1))


def shards(
    axes,
    points,
    ball_ids,
    send_pick,
    recv_from,
    gain_one,
    attn_in_one,
    attn_out_one,
    gain_two,
    mlp_up,
    mlp_down,
    gain_three,
    compress_proj,
    attn_in_two,
    attn_out_two,
):
    peers = axes[1][1]
    cap = send_pick.shape[1] // peers
    width = points.shape[1]
    gains = tuple(g.reshape(1, -1) for g in (gain_one, gain_two, gain_three))
    weights = (attn_in_one, attn_out_one, mlp_up, mlp_down)

    def travel(blocks, s, home):
        if s == 0:
            return blocks
        pattern = [(i, send_to(i, s, peers)) for i in range(peers)]
        if home:
            pattern = [(b, a) for a, b in pattern]
        return lax.ppermute(blocks, "pts", pattern)

    z, h, pool, *sends = layer_one(peers, cap, send_pick, ball_ids, gains, points, weights)
    arrived = [travel(sends[s], s, False) for s in range(peers)]
    pool, far = lax.optimization_barrier((pool, arrived[: -3 : -1]))
    arrived[-2:] = far[::-1]
    pooled = gather_all(pool, axes)
    arrived, pooled = lax.optimization_barrier((arrived[::-1], pooled))
    bounds = [(0, width)]
    back = []
    for start, columns in bounds:
        mixed = layer_two(peers, cap, start, columns, recv_from, arrived[::-1], attn_in_two)
        back.extend(travel(mixed[s], s, True) for s in range(peers - 1, -1, -1))
    base = compressed(h, z, pooled, compress_proj, attn_in_two, attn_out_two)
    return final(peers, cap, bounds, send_pick, back, attn_out_two, base)


def solution(mesh):
    rows = P(("grp", "pts"), None)
    axes = (("grp", mesh.shape["grp"]), ("pts", mesh.shape["pts"]))
    return jax.shard_map(
        partial(shards, axes),
        mesh=mesh,
        in_specs=(rows,) * 4 + (P(),) * 10,
        out_specs=rows,
        check_vma=False,
    )
```

```python
from functools import partial
import math

import jax
import jax.numpy as jnp
from jax import lax
from jax.experimental import pallas as pl
from jax.experimental.pallas import tpu as pltpu
from jax.sharding import PartitionSpec as P

HEAD = 64
LEAF = 128
BALL = 512
CMP = 256
PAIR = 2 * HEAD
HIDE = 512
CHUNK = 256
TILE = 16
MIB = 1 << 20
LATER = 40 * MIB
F32 = jnp.float32
BF16 = jnp.bfloat16
SCALE = HEAD ** (-0.5) * math.log2(math.e)

ANY = pl.BlockSpec(memory_space=pl.ANY)
VMEM = pl.BlockSpec(memory_space=pltpu.VMEM)
SMEM = pl.BlockSpec(memory_space=pltpu.SMEM)


def norm(values, gain):
    wide = values.astype(F32)
    return wide * lax.rsqrt(jnp.mean(wide * wide, axis=-1, keepdims=True) + 1e-06) * gain


def gelu(x):
    c = math.sqrt(2.0 / math.pi)
    t = jnp.tanh(x * (c + (c * 0.044715) * (x * x)))
    return x * (0.5 + 0.5 * t)


def dot(a, b):
    return jnp.dot(a, b, preferred_element_type=F32)


def dot_t(a, b):
    return lax.dot_general(a, b, (((1,), (1,)), ((), ())), preferred_element_type=F32)


def aligned(index, size):
    return pl.ds(pl.multiple_of(index * size, size), size)


def only_head(pair, half):
    lane = lax.broadcasted_iota(jnp.int32, pair.shape, 1)
    return jnp.where((lane >= HEAD) == bool(half), pair, jnp.zeros_like(pair))


def pair_scores(queries, keys):
    both = jnp.concatenate([only_head(queries, 0), only_head(queries, 1)], axis=0)
    return dot_t(both, keys)


def lay_values(out, values):
    keys = values.shape[0]
    ones = jnp.ones_like(values)
    for half in range(2):
        rows = slice(half * keys, (half + 1) * keys)
        out[rows, :PAIR] = only_head(values, half)
        out[rows, PAIR:] = only_head(ones, half)


def weigh(scores, laid):
    rows = scores.shape[0] // 2
    parts = []
    for half in range(2):
        own = scores[half * rows : (half + 1) * rows]
        parts.append(jnp.exp2(own - jnp.max(own, axis=1, keepdims=True)).astype(BF16))
    mixed = dot(jnp.concatenate(parts, axis=1), laid)
    return mixed[:, :PAIR] / mixed[:, PAIR:]


def pipelined(items, first, second):
    held = first(items[0])
    for n, item in enumerate(items):
        now = held
        if n + 1 < len(items):
            held = first(items[n + 1])
        second(item, now)


def send_to(me, s, peers):
    return me ^ s if peers & (peers - 1) == 0 else (me + s) % peers


def got_from(me, s, peers):
    return me ^ s if peers & (peers - 1) == 0 else (me + peers - s) % peers


def start_all(copies):
    for copy in copies:
        copy.start()


def wait_all(copies):
    for copy in copies:
        copy.wait()


def feed_forward(y, gain2, gain3, up_s, down_s):
    inner = norm(y, gain2[...]).astype(BF16)
    total = y.astype(F32)
    for c in range(up_s.shape[1] // HIDE):
        cols = slice(c * HIDE, (c + 1) * HIDE)
        up = gelu(dot(inner, up_s[:, cols])).astype(BF16)
        total = total + dot(up, down_s[cols, :])
    z = total.astype(BF16)
    return z, norm(z, gain3[...]).astype(BF16)


def layer_one_kernel(peers, cap, *refs):
    pick_ref, ids, gain1, gain2, gain3, points, w_in, w_out, w_up, w_down = refs[:10]
    z_out, h_out = refs[10:12]
    sends, refs = refs[12 : 12 + peers], refs[12 + peers :]
    x_s, in_s, wo_s, up_s, down_s, q_s, k_s, v_s, bias_s, mix_s, y_s, z_s, h_s, p_s, sem, send_sem = refs
    me = lax.axis_index("pts").astype(jnp.int32)
    count, width = x_s.shape
    balls = count // BALL
    pairs = width // PAIR
    blocks = count // LEAF
    copies = [
        pltpu.make_async_copy(points, x_s, sem.at[0]),
        pltpu.make_async_copy(w_in, in_s, sem.at[1]),
        pltpu.make_async_copy(w_out, wo_s, sem.at[2]),
        pltpu.make_async_copy(w_up, up_s, sem.at[3]),
        pltpu.make_async_copy(w_down, down_s, sem.at[4]),
    ]
    start_all(copies)
    for b in range(balls):
        across = jnp.broadcast_to(ids[b : b + 1, :], (LEAF, BALL)).astype(F32)
        down = across.T
        for c in range(BALL // LEAF):
            cols = slice(c * LEAF, (c + 1) * LEAF)
            bias_s[b, :, cols] = jnp.where(down == across[:1, cols], 0.0, -1e30)
    copies[0].wait()
    for b in range(balls):
        rows = slice(b * BALL, (b + 1) * BALL)
        h1 = norm(x_s[rows, :], gain1[...]).astype(BF16)
        if b == 0:
            copies[1].wait()
        q_s[rows, :] = (dot(h1, in_s[:, :width]) * SCALE).astype(BF16)
        k_s[rows, :] = dot(h1, in_s[:, width : 2 * width]).astype(BF16)
        values = dot(h1, in_s[:, 2 * width :]).astype(BF16)
        for g in range(pairs):
            lay_values(v_s.at[b * pairs + g], values[:, g * PAIR : (g + 1) * PAIR])

    def scores(item):
        b, g, c = item
        cols = slice(g * PAIR, (g + 1) * PAIR)
        at = b * BALL + c * CHUNK
        return pair_scores(q_s[at : at + CHUNK, cols], k_s[b * BALL : (b + 1) * BALL, cols])

    def mix(item, got):
        b, g, c = item
        at = b * BALL + c * CHUNK
        bias = bias_s[b, c * CHUNK : (c + 1) * CHUNK, :]
        out = weigh(got + jnp.concatenate([bias, bias], axis=0), v_s[b * pairs + g])
        mix_s[at : at + CHUNK, g * PAIR : (g + 1) * PAIR] = out.astype(BF16)

    pipelined(
        [(b, g, c) for b in range(balls) for g in range(pairs) for c in range(BALL // CHUNK)], scores, mix
    )
    copies[2].wait()
    for b in range(balls):
        rows = slice(b * BALL, (b + 1) * BALL)
        y_s[rows, :] = (x_s[rows, :].astype(F32) + dot(mix_s[rows, :], wo_s[...])).astype(BF16)
    copies[3].wait()
    copies[4].wait()
    outgoing, pooled = [], []
    for b in range(balls):
        rows = slice(b * BALL, (b + 1) * BALL)
        z, h3 = feed_forward(y_s[rows, :], gain2, gain3, up_s, down_s)
        z_s[rows, :] = z
        h_s[rows, :] = h3
        wide = h3.astype(F32)
        for c in range(BALL // CMP):
            pooled.append(jnp.sum(wide[c * CMP : (c + 1) * CMP], axis=0, keepdims=True) * CMP ** (-0.5))
        at = pl.ds(b * BALL, BALL)
        for n, (source, there) in enumerate(((z_s, z_out), (h_s, h_out))):
            copy = pltpu.make_async_copy(source.at[at, :], there.at[at, :], sem.at[5 + 2 * b + n])
            copy.start()
            outgoing.append(copy)
    row = lax.broadcasted_iota(jnp.int32, p_s.shape, 0)
    small = jnp.zeros(p_s.shape, F32)
    for i, part in enumerate(pooled):
        small = jnp.where(row == i, part, small)
    p_s[...] = small.astype(BF16)
    for s in range(peers - 1, -1, -1):
        there = sends[s].at[pl.ds(cap * LEAF, p_s.shape[0]), :]
        copy = pltpu.make_async_copy(p_s, there, send_sem.at[peers * cap + s])
        copy.start()
        outgoing.append(copy)
        for c in range(cap):
            slot = send_to(me, s, peers) * cap + c
            block = jnp.minimum(pick_ref[0, slot], blocks - 1)
            there = sends[s].at[pl.ds(c * LEAF, LEAF), :]
            copy = pltpu.make_async_copy(h_s.at[aligned(block, LEAF), :], there, send_sem.at[s * cap + c])
            copy.start()
            outgoing.append(copy)
    wait_all(outgoing)


def layer_one(peers, cap, pick, ids, gains, points, weights):
    count, width = points.shape
    hidden = weights[2].shape[1]
    whole = jax.ShapeDtypeStruct((count, width), BF16)
    tail = -(-(count // CMP) // TILE) * TILE
    block = jax.ShapeDtypeStruct((cap * LEAF + tail, width), BF16)
    balls = count // BALL
    return pl.pallas_call(
        partial(layer_one_kernel, peers, cap),
        out_shape=[whole, whole] + [block] * peers,
        in_specs=[SMEM] + [VMEM] * 4 + [ANY] * 5,
        out_specs=[ANY, ANY] + [ANY] * peers,
        scratch_shapes=[
            pltpu.VMEM((count, width), BF16),
            pltpu.VMEM((width, 3 * width), BF16),
            pltpu.VMEM((width, width), BF16),
            pltpu.VMEM((width, hidden), BF16),
            pltpu.VMEM((hidden, width), BF16),
            pltpu.VMEM((count, width), BF16),
            pltpu.VMEM((count, width), BF16),
            pltpu.VMEM((balls * width // PAIR, 2 * BALL, 2 * PAIR), BF16),
            pltpu.VMEM((balls, BALL, BALL), F32),
            pltpu.VMEM((count, width), BF16),
            pltpu.VMEM((count, width), BF16),
            pltpu.VMEM((count, width), BF16),
            pltpu.VMEM((count, width), BF16),
            pltpu.VMEM((tail, width), BF16),
            pltpu.SemaphoreType.DMA((5 + 2 * balls,)),
            pltpu.SemaphoreType.DMA((peers * (cap + 1),)),
        ],
        compiler_params=pltpu.CompilerParams(vmem_limit_bytes=60 * MIB),
        cost_estimate=pl.CostEstimate(
            flops=count * width * (8 * width + 4 * hidden + 16 * BALL),
            bytes_accessed=10 * MIB,
            transcendentals=count * BALL * width // HEAD,
        ),
        name="layer_one",
    )(pick, ids, *gains, points, *weights)


def place_of(recv_ref, slot, blocks):
    place, found = jnp.int32(0), jnp.int32(0)
    for j in range(blocks):
        hit = (recv_ref[0, j] == slot).astype(jnp.int32)
        place = place + j * hit
        found = found + hit
    return place, found > 0


def layer_two_kernel(peers, cap, blocks, start, columns, *refs):
    recv_ref = refs[0]
    arrived = refs[1 : 1 + peers][::-1]
    w_in = refs[1 + peers]
    outs = refs[2 + peers : 2 + 2 * peers]
    h_s, w_s, q_s, k_s, v_s, a_s, sem, block_sem = refs[2 + 2 * peers :]
    width = h_s.shape[1]
    pairs = columns // PAIR
    me = lax.axis_index("pts").astype(jnp.int32)
    balls = blocks * LEAF // BALL
    copies = []
    for i in range(3):
        cols = pl.ds(i * width + start, columns)
        copies.append(
            pltpu.make_async_copy(w_in.at[:, cols], w_s.at[:, pl.ds(i * columns, columns)], sem.at[i])
        )
    start_all(copies)
    places, moves = [], []
    for s in range(peers):
        for c in range(cap):
            place, found = place_of(recv_ref, got_from(me, s, peers) * cap + c, blocks)
            at = pl.ds(c * LEAF, LEAF)
            move = pltpu.make_async_copy(
                arrived[s].at[at, :], h_s.at[aligned(place, LEAF), :], block_sem.at[s * cap + c]
            )
            places.append(place)
            moves.append((found, move))
            pl.when(found)(move.start)
    wait_all(copies)
    for found, move in moves:
        pl.when(found)(move.wait)
    for b in range(balls):
        rows = slice(b * BALL, (b + 1) * BALL)
        h = h_s[rows, :]
        q_s[rows, :] = (dot(h, w_s[:, :columns]) * SCALE).astype(BF16)
        k_s[rows, :] = dot(h, w_s[:, columns : 2 * columns]).astype(BF16)
        values = dot(h, w_s[:, 2 * columns :]).astype(BF16)
        for g in range(pairs):
            lay_values(v_s.at[b * pairs + g], values[:, g * PAIR : (g + 1) * PAIR])

    def scores(item):
        b, g, c = item
        cols = slice(g * PAIR, (g + 1) * PAIR)
        at = b * BALL + c * CHUNK
        return pair_scores(q_s[at : at + CHUNK, cols], k_s[b * BALL : (b + 1) * BALL, cols])

    def mix(item, got):
        b, g, c = item
        at = b * BALL + c * CHUNK
        a_s[at : at + CHUNK, g * PAIR : (g + 1) * PAIR] = weigh(got, v_s[b * pairs + g]).astype(BF16)

    pipelined(
        [(b, g, c) for b in range(balls) for g in range(pairs) for c in range(BALL // CHUNK)], scores, mix
    )
    outgoing = []
    for s in range(peers):
        for c in range(cap):
            n = s * cap + c
            at = pl.ds(c * LEAF, LEAF)
            outgoing.append(
                pltpu.make_async_copy(a_s.at[aligned(places[n], LEAF), :], outs[s].at[at, :], block_sem.at[n])
            )
    start_all(outgoing)
    wait_all(outgoing)


def layer_two(peers, cap, start, columns, recv, arrived, w_in):
    blocks = recv.shape[1]
    width = w_in.shape[0]
    pairs = columns // PAIR
    rows = blocks * LEAF
    block = jax.ShapeDtypeStruct((cap * LEAF, columns), BF16)
    return pl.pallas_call(
        partial(layer_two_kernel, peers, cap, blocks, start, columns),
        out_shape=[block] * peers,
        in_specs=[SMEM] + [ANY] * (peers + 1),
        out_specs=[ANY] * peers,
        scratch_shapes=[
            pltpu.VMEM((rows, width), BF16),
            pltpu.VMEM((width, 3 * columns), BF16),
            pltpu.VMEM((rows, columns), BF16),
            pltpu.VMEM((rows, columns), BF16),
            pltpu.VMEM((rows // BALL * pairs, 2 * BALL, 2 * PAIR), BF16),
            pltpu.VMEM((rows, columns), BF16),
            pltpu.SemaphoreType.DMA((3,)),
            pltpu.SemaphoreType.DMA((peers * cap,)),
        ],
        compiler_params=pltpu.CompilerParams(vmem_limit_bytes=LATER),
        cost_estimate=pl.CostEstimate(
            flops=rows * columns * (6 * width + 16 * BALL),
            bytes_accessed=4 * MIB,
            transcendentals=rows * BALL * columns // HEAD,
        ),
        name=f"layer_two_{start}",
    )(recv, *arrived[::-1], w_in)


def compressed_kernel(slabs, tail, local, *refs):
    pools = refs[:slabs]
    h, z, w_comp, w_in, w_out, out = refs[slabs : slabs + 6]
    h_s, z_s, p_s, wc_s, wq_s, wo_s, q_s, ck_s, cv_s, a_s, o_s, sem, pool_sem, out_sem = refs[slabs + 6 :]
    rows, width = h_s.shape
    pairs = width // PAIR
    comp = ck_s.shape[0]
    copies = [
        pltpu.make_async_copy(w_comp, wc_s, sem.at[0]),
        pltpu.make_async_copy(w_in.at[:, pl.ds(0, width)], wq_s, sem.at[1]),
        pltpu.make_async_copy(h, h_s, sem.at[2]),
        pltpu.make_async_copy(w_out, wo_s, sem.at[3]),
        pltpu.make_async_copy(z, z_s, sem.at[4]),
    ]
    small = []
    for n, pool in enumerate(pools):
        there = p_s.at[pl.ds(n * pool.shape[0], pool.shape[0]), :]
        small.append(pltpu.make_async_copy(pool, there, pool_sem.at[n]))
    start_all(small)
    start_all(copies)
    key = lax.broadcasted_iota(jnp.int32, (comp, p_s.shape[0]), 0)
    at = lax.broadcasted_iota(jnp.int32, (comp, p_s.shape[0]), 1)
    taken = jnp.where(at == key // local * tail + key % local, 1.0, 0.0).astype(BF16)
    wait_all(small)
    pooled = dot(taken, p_s[...]).astype(BF16)
    copies[0].wait()
    far = dot(pooled, wc_s[...]).astype(BF16)
    ck_s[...] = far[:, :width]
    for g in range(pairs):
        lay_values(cv_s.at[g], far[:, width + g * PAIR : width + (g + 1) * PAIR])
    wait_all(copies[1:3])
    q_s[...] = (dot(h_s[...], wq_s[...]) * SCALE).astype(BF16)

    def scores(item):
        g, c = item
        cols = slice(g * PAIR, (g + 1) * PAIR)
        return pair_scores(q_s[c * CHUNK : (c + 1) * CHUNK, cols], ck_s[:, cols])

    def mix(item, got):
        g, c = item
        a_s[c * CHUNK : (c + 1) * CHUNK, g * PAIR : (g + 1) * PAIR] = weigh(got, cv_s[g]).astype(BF16)

    pipelined([(g, c) for c in range(rows // CHUNK) for g in range(pairs)], scores, mix)
    wait_all(copies[3:])
    outgoing = []
    for c in range(rows // CHUNK):
        at = slice(c * CHUNK, (c + 1) * CHUNK)
        o_s[at, :] = z_s[at, :].astype(F32) + dot(a_s[at, :], wo_s[...])
        there = pl.ds(c * CHUNK, CHUNK)
        copy = pltpu.make_async_copy(o_s.at[there, :], out.at[there, :], out_sem.at[c])
        copy.start()
        outgoing.append(copy)
    wait_all(outgoing)


def compressed(tail, local, pools, h, z, w_comp, w_in, w_out):
    rows, width = h.shape
    held = sum(p.shape[0] for p in pools)
    comp = held // tail * local
    return pl.pallas_call(
        partial(compressed_kernel, len(pools), tail, local),
        out_shape=jax.ShapeDtypeStruct((rows, width), F32),
        in_specs=[ANY] * (5 + len(pools)),
        out_specs=ANY,
        scratch_shapes=[
            pltpu.VMEM((rows, width), BF16),
            pltpu.VMEM((rows, width), BF16),
            pltpu.VMEM((held, width), BF16),
            pltpu.VMEM((width, 2 * width), BF16),
            pltpu.VMEM((width, width), BF16),
            pltpu.VMEM((width, width), BF16),
            pltpu.VMEM((rows, width), BF16),
            pltpu.VMEM((comp, width), BF16),
            pltpu.VMEM((width // PAIR, 2 * comp, 2 * PAIR), BF16),
            pltpu.VMEM((rows, width), BF16),
            pltpu.VMEM((rows, width), F32),
            pltpu.SemaphoreType.DMA((5,)),
            pltpu.SemaphoreType.DMA((len(pools),)),
            pltpu.SemaphoreType.DMA((rows // CHUNK,)),
        ],
        compiler_params=pltpu.CompilerParams(vmem_limit_bytes=LATER),
        cost_estimate=pl.CostEstimate(
            flops=rows * width * (4 * width + 16 * comp),
            bytes_accessed=8 * MIB,
            transcendentals=rows * comp * width // HEAD,
        ),
        name="compressed",
    )(*pools, h, z, w_comp, w_in, w_out)


def final_kernel(peers, cap, bounds, pick_ref, *refs):
    parts = len(bounds)
    back = [refs[p * peers : (p + 1) * peers][::-1] for p in range(parts)]
    w_out, base, out, w_s, b_s, m_s, o_s, sem, block_sem, out_sem = refs[parts * peers :]
    blocks = b_s.shape[0] // LEAF
    me = lax.axis_index("pts").astype(jnp.int32)
    copies = [
        pltpu.make_async_copy(w_out, w_s, sem.at[0]),
        pltpu.make_async_copy(base, b_s, sem.at[1]),
    ]
    start_all(copies)
    moves = []
    for p, (start, columns) in enumerate(bounds):
        for s in range(peers):
            for c in range(cap):
                block = pick_ref[0, send_to(me, s, peers) * cap + c]
                found = block < blocks
                at = pl.ds(c * LEAF, LEAF)
                place = aligned(jnp.minimum(block, blocks - 1), LEAF)
                move = pltpu.make_async_copy(
                    back[p][s].at[at, :],
                    m_s.at[place, pl.ds(start, columns)],
                    block_sem.at[(p * peers + s) * cap + c],
                )
                moves.append((found, move))
                pl.when(found)(move.start)
    wait_all(copies)
    for found, move in moves:
        pl.when(found)(move.wait)
    outgoing = []
    for b in range(b_s.shape[0] // CHUNK):
        rows = slice(b * CHUNK, (b + 1) * CHUNK)
        o_s[rows, :] = (b_s[rows, :] + dot(m_s[rows, :], w_s[...])).astype(BF16)
        at = pl.ds(b * CHUNK, CHUNK)
        copy = pltpu.make_async_copy(o_s.at[at, :], out.at[at, :], out_sem.at[b])
        copy.start()
        outgoing.append(copy)
    wait_all(outgoing)


def final(peers, cap, bounds, pick, back, w_out, base):
    rows, width = base.shape
    return pl.pallas_call(
        partial(final_kernel, peers, cap, bounds),
        out_shape=jax.ShapeDtypeStruct((rows, width), BF16),
        in_specs=[SMEM] + [ANY] * (peers * len(bounds) + 2),
        out_specs=ANY,
        scratch_shapes=[
            pltpu.VMEM((width, width), BF16),
            pltpu.VMEM((rows, width), F32),
            pltpu.VMEM((rows, width), BF16),
            pltpu.VMEM((rows, width), BF16),
            pltpu.SemaphoreType.DMA((2,)),
            pltpu.SemaphoreType.DMA((len(bounds) * peers * cap,)),
            pltpu.SemaphoreType.DMA((rows // CHUNK,)),
        ],
        compiler_params=pltpu.CompilerParams(vmem_limit_bytes=LATER),
        cost_estimate=pl.CostEstimate(
            flops=2 * rows * width * width, bytes_accessed=4 * MIB, transcendentals=0
        ),
        name="last_product",
    )(pick, *back, w_out, base)


def shards(
    axes,
    points,
    ball_ids,
    send_pick,
    recv_from,
    gain_one,
    attn_in_one,
    attn_out_one,
    gain_two,
    mlp_up,
    mlp_down,
    gain_three,
    compress_proj,
    attn_in_two,
    attn_out_two,
):
    peers = axes[1][1]
    cap = send_pick.shape[1] // peers
    width = points.shape[1]
    gains = tuple(g.reshape(1, -1) for g in (gain_one, gain_two, gain_three))
    weights = (attn_in_one, attn_out_one, mlp_up, mlp_down)

    def travel(blocks, s, home):
        if s == 0:
            return blocks
        pattern = [(i, send_to(i, s, peers)) for i in range(peers)]
        if home:
            pattern = [(b, a) for a, b in pattern]
        return lax.ppermute(blocks, "pts", pattern)

    z, h, *sends = layer_one(peers, cap, send_pick, ball_ids, gains, points, weights)
    arrived = [travel(sends[s], s, False) for s in range(peers)]
    tail = sends[0].shape[0] - cap * LEAF
    slab = jnp.concatenate([block[cap * LEAF :] for block in arrived])
    groups = axes[0][1]
    turns = [[(i, (i + s) % groups) for i in range(groups)] for s in range(1, groups)]
    pools = [slab] + [lax.ppermute(slab, "grp", turn) for turn in turns]
    mixed = layer_two(peers, cap, 0, width, recv_from, arrived, attn_in_two)
    mixed, pools = lax.optimization_barrier((mixed, pools))
    bounds = [(0, width)]
    back = [travel(mixed[s], s, True) for s in range(peers - 1, -1, -1)]
    local = points.shape[0] // CMP
    base = compressed(tail, local, pools, h, z, compress_proj, attn_in_two, attn_out_two)
    return final(peers, cap, bounds, send_pick, back, attn_out_two, base)


def solution(mesh):
    rows = P(("grp", "pts"), None)
    axes = (("grp", mesh.shape["grp"]), ("pts", mesh.shape["pts"]))
    return jax.shard_map(
        partial(shards, axes),
        mesh=mesh,
        in_specs=(rows,) * 4 + (P(),) * 10,
        out_specs=rows,
        check_vma=False,
    )
```

```python
from functools import partial
import math

import jax
import jax.numpy as jnp
from jax import lax
from jax.experimental import pallas as pl
from jax.experimental.pallas import tpu as pltpu
from jax.sharding import PartitionSpec as P

HEAD = 64
LEAF = 128
BALL = 512
CMP = 256
PAIR = 2 * HEAD
HIDE = 512
CHUNK = 256
TILE = 16
MIB = 1 << 20
LATER = 40 * MIB
F32 = jnp.float32
BF16 = jnp.bfloat16
SCALE = HEAD ** (-0.5) * math.log2(math.e)

ANY = pl.BlockSpec(memory_space=pl.ANY)
VMEM = pl.BlockSpec(memory_space=pltpu.VMEM)
SMEM = pl.BlockSpec(memory_space=pltpu.SMEM)


def norm(values, gain):
    wide = values.astype(F32)
    return wide * lax.rsqrt(jnp.mean(wide * wide, axis=-1, keepdims=True) + 1e-06) * gain


def gelu(x):
    c = math.sqrt(2.0 / math.pi)
    t = jnp.tanh(x * (c + (c * 0.044715) * (x * x)))
    return x * (0.5 + 0.5 * t)


def dot(a, b):
    return jnp.dot(a, b, preferred_element_type=F32)


def dot_t(a, b):
    return lax.dot_general(a, b, (((1,), (1,)), ((), ())), preferred_element_type=F32)


def aligned(index, size):
    return pl.ds(pl.multiple_of(index * size, size), size)


def only_head(pair, half):
    lane = lax.broadcasted_iota(jnp.int32, pair.shape, 1)
    return jnp.where((lane >= HEAD) == bool(half), pair, jnp.zeros_like(pair))


def pair_scores(queries, keys):
    both = jnp.concatenate([only_head(queries, 0), only_head(queries, 1)], axis=0)
    return dot_t(both, keys)


def lay_values(out, values):
    keys = values.shape[0]
    ones = jnp.ones_like(values)
    for half in range(2):
        rows = slice(half * keys, (half + 1) * keys)
        out[rows, :PAIR] = only_head(values, half)
        out[rows, PAIR:] = only_head(ones, half)


def weigh(scores, laid):
    rows = scores.shape[0] // 2
    parts = []
    for half in range(2):
        own = scores[half * rows : (half + 1) * rows]
        parts.append(jnp.exp2(own - jnp.max(own, axis=1, keepdims=True)).astype(BF16))
    mixed = dot(jnp.concatenate(parts, axis=1), laid)
    return mixed[:, :PAIR] / mixed[:, PAIR:]


def pipelined(items, first, second):
    held = first(items[0])
    for n, item in enumerate(items):
        now = held
        if n + 1 < len(items):
            held = first(items[n + 1])
        second(item, now)


def send_to(me, s, peers):
    return me ^ s if peers & (peers - 1) == 0 else (me + s) % peers


def got_from(me, s, peers):
    return me ^ s if peers & (peers - 1) == 0 else (me + peers - s) % peers


def start_all(copies):
    for copy in copies:
        copy.start()


def wait_all(copies):
    for copy in copies:
        copy.wait()


def feed_forward(y, gain2, gain3, up_s, down_s):
    inner = norm(y, gain2[...]).astype(BF16)
    total = [y.astype(F32)]

    def rise(c):
        return dot(inner, up_s[:, c * HIDE : (c + 1) * HIDE])

    def fall(c, got):
        total[0] = total[0] + dot(gelu(got).astype(BF16), down_s[c * HIDE : (c + 1) * HIDE, :])

    pipelined(list(range(up_s.shape[1] // HIDE)), rise, fall)
    z = total[0].astype(BF16)
    return z, norm(z, gain3[...]).astype(BF16)


def layer_one_kernel(peers, cap, *refs):
    pick_ref, ids, gain1, gain2, gain3, points, w_in, w_out, w_up, w_down = refs[:10]
    z_out, h_out = refs[10:12]
    sends, refs = refs[12 : 12 + peers], refs[12 + peers :]
    x_s, in_s, wo_s, up_s, down_s, q_s, k_s, v_s, bias_s, mix_s, y_s, z_s, h_s, p_s, sem, send_sem = refs
    me = lax.axis_index("pts").astype(jnp.int32)
    count, width = x_s.shape
    balls = count // BALL
    pairs = width // PAIR
    blocks = count // LEAF
    copies = [
        pltpu.make_async_copy(points, x_s, sem.at[0]),
        pltpu.make_async_copy(w_in, in_s, sem.at[1]),
        pltpu.make_async_copy(w_out, wo_s, sem.at[2]),
        pltpu.make_async_copy(w_up, up_s, sem.at[3]),
        pltpu.make_async_copy(w_down, down_s, sem.at[4]),
    ]
    start_all(copies[:2])
    for b in range(balls):
        across = jnp.broadcast_to(ids[b : b + 1, :], (LEAF, BALL)).astype(F32)
        down = across.T
        for c in range(BALL // LEAF):
            cols = slice(c * LEAF, (c + 1) * LEAF)
            bias_s[b, :, cols] = jnp.where(down == across[:1, cols], 0.0, -1e30)
    copies[0].wait()
    for b in range(balls):
        rows = slice(b * BALL, (b + 1) * BALL)
        h1 = norm(x_s[rows, :], gain1[...]).astype(BF16)
        if b == 0:
            copies[1].wait()
            start_all(copies[2:])
        q_s[rows, :] = (dot(h1, in_s[:, :width]) * SCALE).astype(BF16)
        k_s[rows, :] = dot(h1, in_s[:, width : 2 * width]).astype(BF16)
        values = dot(h1, in_s[:, 2 * width :]).astype(BF16)
        for g in range(pairs):
            lay_values(v_s.at[b * pairs + g], values[:, g * PAIR : (g + 1) * PAIR])

    def scores(item):
        b, g, c = item
        cols = slice(g * PAIR, (g + 1) * PAIR)
        at = b * BALL + c * CHUNK
        return pair_scores(q_s[at : at + CHUNK, cols], k_s[b * BALL : (b + 1) * BALL, cols])

    def mix(item, got):
        b, g, c = item
        at = b * BALL + c * CHUNK
        bias = bias_s[b, c * CHUNK : (c + 1) * CHUNK, :]
        out = weigh(got + jnp.concatenate([bias, bias], axis=0), v_s[b * pairs + g])
        mix_s[at : at + CHUNK, g * PAIR : (g + 1) * PAIR] = out.astype(BF16)

    pipelined(
        [(b, g, c) for b in range(balls) for g in range(pairs) for c in range(BALL // CHUNK)], scores, mix
    )
    copies[2].wait()
    for b in range(balls):
        rows = slice(b * BALL, (b + 1) * BALL)
        y_s[rows, :] = (x_s[rows, :].astype(F32) + dot(mix_s[rows, :], wo_s[...])).astype(BF16)
    copies[3].wait()
    copies[4].wait()
    outgoing, pooled = [], []
    for b in range(balls):
        rows = slice(b * BALL, (b + 1) * BALL)
        z, h3 = feed_forward(y_s[rows, :], gain2, gain3, up_s, down_s)
        z_s[rows, :] = z
        h_s[rows, :] = h3
        wide = h3.astype(F32)
        for c in range(BALL // CMP):
            pooled.append(jnp.sum(wide[c * CMP : (c + 1) * CMP], axis=0, keepdims=True) * CMP ** (-0.5))
        at = pl.ds(b * BALL, BALL)
        for n, (source, there) in enumerate(((z_s, z_out), (h_s, h_out))):
            copy = pltpu.make_async_copy(source.at[at, :], there.at[at, :], sem.at[5 + 2 * b + n])
            copy.start()
            outgoing.append(copy)
    row = lax.broadcasted_iota(jnp.int32, p_s.shape, 0)
    small = jnp.zeros(p_s.shape, F32)
    for i, part in enumerate(pooled):
        small = jnp.where(row == i, part, small)
    p_s[...] = small.astype(BF16)
    for s in range(peers - 1, -1, -1):
        there = sends[s].at[pl.ds(cap * LEAF, p_s.shape[0]), :]
        copy = pltpu.make_async_copy(p_s, there, send_sem.at[peers * cap + s])
        copy.start()
        outgoing.append(copy)
        for c in range(cap):
            slot = send_to(me, s, peers) * cap + c
            block = jnp.minimum(pick_ref[0, slot], blocks - 1)
            there = sends[s].at[pl.ds(c * LEAF, LEAF), :]
            copy = pltpu.make_async_copy(h_s.at[aligned(block, LEAF), :], there, send_sem.at[s * cap + c])
            copy.start()
            outgoing.append(copy)
    wait_all(outgoing)


def layer_one(peers, cap, pick, ids, gains, points, weights):
    count, width = points.shape
    hidden = weights[2].shape[1]
    whole = jax.ShapeDtypeStruct((count, width), BF16)
    tail = -(-(count // CMP) // TILE) * TILE
    block = jax.ShapeDtypeStruct((cap * LEAF + tail, width), BF16)
    balls = count // BALL
    return pl.pallas_call(
        partial(layer_one_kernel, peers, cap),
        out_shape=[whole, whole] + [block] * peers,
        in_specs=[SMEM] + [VMEM] * 4 + [ANY] * 5,
        out_specs=[ANY, ANY] + [ANY] * peers,
        scratch_shapes=[
            pltpu.VMEM((count, width), BF16),
            pltpu.VMEM((width, 3 * width), BF16),
            pltpu.VMEM((width, width), BF16),
            pltpu.VMEM((width, hidden), BF16),
            pltpu.VMEM((hidden, width), BF16),
            pltpu.VMEM((count, width), BF16),
            pltpu.VMEM((count, width), BF16),
            pltpu.VMEM((balls * width // PAIR, 2 * BALL, 2 * PAIR), BF16),
            pltpu.VMEM((balls, BALL, BALL), F32),
            pltpu.VMEM((count, width), BF16),
            pltpu.VMEM((count, width), BF16),
            pltpu.VMEM((count, width), BF16),
            pltpu.VMEM((count, width), BF16),
            pltpu.VMEM((tail, width), BF16),
            pltpu.SemaphoreType.DMA((5 + 2 * balls,)),
            pltpu.SemaphoreType.DMA((peers * (cap + 1),)),
        ],
        compiler_params=pltpu.CompilerParams(vmem_limit_bytes=60 * MIB),
        cost_estimate=pl.CostEstimate(
            flops=count * width * (8 * width + 4 * hidden + 16 * BALL),
            bytes_accessed=10 * MIB,
            transcendentals=count * BALL * width // HEAD,
        ),
        name="layer_one",
    )(pick, ids, *gains, points, *weights)


def place_of(recv_ref, slot, blocks):
    place, found = jnp.int32(0), jnp.int32(0)
    for j in range(blocks):
        hit = (recv_ref[0, j] == slot).astype(jnp.int32)
        place = place + j * hit
        found = found + hit
    return place, found > 0


def layer_two_kernel(peers, cap, flow, blocks, start, columns, *refs):
    recv_ref = refs[0]
    arrived = dict(zip(flow, refs[1 : 1 + peers]))
    w_in = refs[1 + peers]
    outs = refs[2 + peers : 2 + 2 * peers]
    h_s, q_s, k_s, v_s, a_s = refs[2 + 2 * peers :]
    width = h_s.shape[1]
    pairs = columns // PAIR
    me = lax.axis_index("pts").astype(jnp.int32)
    balls = blocks * LEAF // BALL
    places = []
    for s in range(peers):
        for c in range(cap):
            place, found = place_of(recv_ref, got_from(me, s, peers) * cap + c, blocks)
            places.append(place)

            @pl.when(found)
            def _():
                h_s[aligned(place, LEAF), :] = arrived[s][c * LEAF : (c + 1) * LEAF, :]

    def product(h, i):
        return dot(h, w_in[:, i * width + start : i * width + start + columns])

    for b in range(balls):
        rows = slice(b * BALL, (b + 1) * BALL)
        h = h_s[rows, :]
        q_s[rows, :] = (product(h, 0) * SCALE).astype(BF16)
        k_s[rows, :] = product(h, 1).astype(BF16)
        values = product(h, 2).astype(BF16)
        for g in range(pairs):
            lay_values(v_s.at[b * pairs + g], values[:, g * PAIR : (g + 1) * PAIR])

    def scores(item):
        b, g, c = item
        cols = slice(g * PAIR, (g + 1) * PAIR)
        at = b * BALL + c * CHUNK
        return pair_scores(q_s[at : at + CHUNK, cols], k_s[b * BALL : (b + 1) * BALL, cols])

    def mix(item, got):
        b, g, c = item
        at = b * BALL + c * CHUNK
        a_s[at : at + CHUNK, g * PAIR : (g + 1) * PAIR] = weigh(got, v_s[b * pairs + g]).astype(BF16)

    pipelined(
        [(b, g, c) for b in range(balls) for g in range(pairs) for c in range(BALL // CHUNK)], scores, mix
    )
    for s in range(peers):
        for c in range(cap):
            outs[s][c * LEAF : (c + 1) * LEAF, :] = a_s[aligned(places[s * cap + c], LEAF), :]


def layer_two(peers, cap, flow, start, columns, recv, arrived, w_in):
    blocks = recv.shape[1]
    width = w_in.shape[0]
    pairs = columns // PAIR
    rows = blocks * LEAF
    block = jax.ShapeDtypeStruct((cap * LEAF, columns), BF16)
    return pl.pallas_call(
        partial(layer_two_kernel, peers, cap, flow, blocks, start, columns),
        out_shape=[block] * peers,
        in_specs=[SMEM] + [VMEM] * (peers + 1),
        out_specs=[VMEM] * peers,
        scratch_shapes=[
            pltpu.VMEM((rows, width), BF16),
            pltpu.VMEM((rows, columns), BF16),
            pltpu.VMEM((rows, columns), BF16),
            pltpu.VMEM((rows // BALL * pairs, 2 * BALL, 2 * PAIR), BF16),
            pltpu.VMEM((rows, columns), BF16),
        ],
        compiler_params=pltpu.CompilerParams(vmem_limit_bytes=LATER),
        cost_estimate=pl.CostEstimate(
            flops=rows * columns * (6 * width + 16 * BALL),
            bytes_accessed=4 * MIB,
            transcendentals=rows * BALL * columns // HEAD,
        ),
        name=f"layer_two_{start}",
    )(recv, *[arrived[s] for s in flow], w_in)


def compressed_kernel(slabs, tail, local, *refs):
    pools = refs[:slabs]
    h, z, w_comp, w_in, w_out, out = refs[slabs : slabs + 6]
    h_s, z_s, p_s, wc_s, wq_s, wo_s, q_s, ck_s, cv_s, a_s, o_s, sem, pool_sem, out_sem = refs[slabs + 6 :]
    rows, width = h_s.shape
    pairs = width // PAIR
    comp = ck_s.shape[0]
    copies = [
        pltpu.make_async_copy(w_comp, wc_s, sem.at[0]),
        pltpu.make_async_copy(w_in.at[:, pl.ds(0, width)], wq_s, sem.at[1]),
        pltpu.make_async_copy(h, h_s, sem.at[2]),
        pltpu.make_async_copy(w_out, wo_s, sem.at[3]),
        pltpu.make_async_copy(z, z_s, sem.at[4]),
    ]
    small = []
    for n, pool in enumerate(pools):
        there = p_s.at[pl.ds(n * pool.shape[0], pool.shape[0]), :]
        small.append(pltpu.make_async_copy(pool, there, pool_sem.at[n]))
    start_all(small)
    start_all(copies)
    key = lax.broadcasted_iota(jnp.int32, (comp, p_s.shape[0]), 0)
    at = lax.broadcasted_iota(jnp.int32, (comp, p_s.shape[0]), 1)
    taken = jnp.where(at == key // local * tail + key % local, 1.0, 0.0).astype(BF16)
    wait_all(small)
    pooled = dot(taken, p_s[...]).astype(BF16)
    copies[0].wait()
    far = dot(pooled, wc_s[...]).astype(BF16)
    ck_s[...] = far[:, :width]
    for g in range(pairs):
        lay_values(cv_s.at[g], far[:, width + g * PAIR : width + (g + 1) * PAIR])
    wait_all(copies[1:3])
    q_s[...] = (dot(h_s[...], wq_s[...]) * SCALE).astype(BF16)

    def scores(item):
        g, c = item
        cols = slice(g * PAIR, (g + 1) * PAIR)
        return pair_scores(q_s[c * CHUNK : (c + 1) * CHUNK, cols], ck_s[:, cols])

    def mix(item, got):
        g, c = item
        a_s[c * CHUNK : (c + 1) * CHUNK, g * PAIR : (g + 1) * PAIR] = weigh(got, cv_s[g]).astype(BF16)

    pipelined([(g, c) for c in range(rows // CHUNK) for g in range(pairs)], scores, mix)
    wait_all(copies[3:])
    outgoing = []
    for c in range(rows // CHUNK):
        at = slice(c * CHUNK, (c + 1) * CHUNK)
        o_s[at, :] = z_s[at, :].astype(F32) + dot(a_s[at, :], wo_s[...])
        there = pl.ds(c * CHUNK, CHUNK)
        copy = pltpu.make_async_copy(o_s.at[there, :], out.at[there, :], out_sem.at[c])
        copy.start()
        outgoing.append(copy)
    wait_all(outgoing)


def compressed(tail, local, pools, h, z, w_comp, w_in, w_out):
    rows, width = h.shape
    held = sum(p.shape[0] for p in pools)
    comp = held // tail * local
    return pl.pallas_call(
        partial(compressed_kernel, len(pools), tail, local),
        out_shape=jax.ShapeDtypeStruct((rows, width), F32),
        in_specs=[ANY] * (5 + len(pools)),
        out_specs=ANY,
        scratch_shapes=[
            pltpu.VMEM((rows, width), BF16),
            pltpu.VMEM((rows, width), BF16),
            pltpu.VMEM((held, width), BF16),
            pltpu.VMEM((width, 2 * width), BF16),
            pltpu.VMEM((width, width), BF16),
            pltpu.VMEM((width, width), BF16),
            pltpu.VMEM((rows, width), BF16),
            pltpu.VMEM((comp, width), BF16),
            pltpu.VMEM((width // PAIR, 2 * comp, 2 * PAIR), BF16),
            pltpu.VMEM((rows, width), BF16),
            pltpu.VMEM((rows, width), F32),
            pltpu.SemaphoreType.DMA((5,)),
            pltpu.SemaphoreType.DMA((len(pools),)),
            pltpu.SemaphoreType.DMA((rows // CHUNK,)),
        ],
        compiler_params=pltpu.CompilerParams(vmem_limit_bytes=LATER),
        cost_estimate=pl.CostEstimate(
            flops=rows * width * (4 * width + 16 * comp),
            bytes_accessed=8 * MIB,
            transcendentals=rows * comp * width // HEAD,
        ),
        name="compressed",
    )(*pools, h, z, w_comp, w_in, w_out)


def final_kernel(peers, cap, bounds, pick_ref, *refs):
    parts = len(bounds)
    back = [refs[p * peers : (p + 1) * peers][::-1] for p in range(parts)]
    w_out, base, out, m_s, o_s, out_sem = refs[parts * peers :]
    blocks = base.shape[0] // LEAF
    me = lax.axis_index("pts").astype(jnp.int32)
    for p, (start, columns) in enumerate(bounds):
        for s in range(peers):
            for c in range(cap):
                block = pick_ref[0, send_to(me, s, peers) * cap + c]

                @pl.when(block < blocks)
                def _():
                    got = back[p][s][c * LEAF : (c + 1) * LEAF, :]
                    m_s[aligned(block, LEAF), start : start + columns] = got

    outgoing = []
    for b in range(base.shape[0] // CHUNK):
        rows = slice(b * CHUNK, (b + 1) * CHUNK)
        o_s[rows, :] = (base[rows, :] + dot(m_s[rows, :], w_out[...])).astype(BF16)
        at = pl.ds(b * CHUNK, CHUNK)
        copy = pltpu.make_async_copy(o_s.at[at, :], out.at[at, :], out_sem.at[b])
        copy.start()
        outgoing.append(copy)
    wait_all(outgoing)


def final(peers, cap, bounds, pick, back, w_out, base):
    rows, width = base.shape
    return pl.pallas_call(
        partial(final_kernel, peers, cap, bounds),
        out_shape=jax.ShapeDtypeStruct((rows, width), BF16),
        in_specs=[SMEM] + [VMEM] * (peers * len(bounds) + 2),
        out_specs=ANY,
        scratch_shapes=[
            pltpu.VMEM((rows, width), BF16),
            pltpu.VMEM((rows, width), BF16),
            pltpu.SemaphoreType.DMA((rows // CHUNK,)),
        ],
        compiler_params=pltpu.CompilerParams(vmem_limit_bytes=LATER),
        cost_estimate=pl.CostEstimate(
            flops=2 * rows * width * width, bytes_accessed=4 * MIB, transcendentals=0
        ),
        name="last_product",
    )(pick, *back, w_out, base)


def shards(
    axes,
    points,
    ball_ids,
    send_pick,
    recv_from,
    gain_one,
    attn_in_one,
    attn_out_one,
    gain_two,
    mlp_up,
    mlp_down,
    gain_three,
    compress_proj,
    attn_in_two,
    attn_out_two,
):
    peers = axes[1][1]
    cap = send_pick.shape[1] // peers
    width = points.shape[1]
    gains = tuple(g.reshape(1, -1) for g in (gain_one, gain_two, gain_three))
    weights = (attn_in_one, attn_out_one, mlp_up, mlp_down)

    def travel(blocks, s, home):
        if s == 0:
            return blocks
        pattern = [(i, send_to(i, s, peers)) for i in range(peers)]
        if home:
            pattern = [(b, a) for a, b in pattern]
        return lax.ppermute(blocks, "pts", pattern)

    z, h, *sends = layer_one(peers, cap, send_pick, ball_ids, gains, points, weights)
    arrived = [travel(sends[s], s, False) for s in range(peers)]
    flow = [s for s in (2, 1, *range(peers - 1, 2, -1), 0) if s < peers]
    tail = sends[0].shape[0] - cap * LEAF
    first = [s for s in (1, 2, 3, 0) if s < peers]
    last = list(range(peers - 1, 3, -1))
    slab = jnp.concatenate([arrived[s][cap * LEAF :] for s in first + last])
    groups = axes[0][1]
    turns = [[(i, (i + s) % groups) for i in range(groups)] for s in range(1, groups)]
    pools = [slab] + [lax.ppermute(slab, "grp", turn) for turn in turns]
    mixed = layer_two(peers, cap, flow, 0, width, recv_from, arrived, attn_in_two)
    mixed, pools = lax.optimization_barrier((mixed, pools))
    bounds = [(0, width)]
    back = [travel(mixed[s], s, True) for s in range(peers - 1, -1, -1)]
    local = points.shape[0] // CMP
    base = compressed(tail, local, pools, h, z, compress_proj, attn_in_two, attn_out_two)
    return final(peers, cap, bounds, send_pick, back, attn_out_two, base)


def solution(mesh):
    rows = P(("grp", "pts"), None)
    axes = (("grp", mesh.shape["grp"]), ("pts", mesh.shape["pts"]))
    return jax.shard_map(
        partial(shards, axes),
        mesh=mesh,
        in_specs=(rows,) * 4 + (P(),) * 10,
        out_specs=rows,
        check_vma=False,
    )
```

```python
from functools import partial
import math

import jax
import jax.numpy as jnp
from jax import lax
from jax.experimental import pallas as pl
from jax.experimental.pallas import tpu as pltpu
from jax.sharding import PartitionSpec as P

HEAD = 64
LEAF = 128
BALL = 512
CMP = 256
PAIR = 2 * HEAD
HIDE = 512
CHUNK = 256
TILE = 16
MIB = 1 << 20
LATER = 40 * MIB
F32 = jnp.float32
BF16 = jnp.bfloat16
SCALE = HEAD ** (-0.5) * math.log2(math.e)

ANY = pl.BlockSpec(memory_space=pl.ANY)
VMEM = pl.BlockSpec(memory_space=pltpu.VMEM)
SMEM = pl.BlockSpec(memory_space=pltpu.SMEM)


def norm(values, gain):
    wide = values.astype(F32)
    return wide * lax.rsqrt(jnp.mean(wide * wide, axis=-1, keepdims=True) + 1e-06) * gain


def gelu(x):
    c = math.sqrt(2.0 / math.pi)
    t = jnp.tanh(x * (c + (c * 0.044715) * (x * x)))
    return x * (0.5 + 0.5 * t)


def dot(a, b):
    return jnp.dot(a, b, preferred_element_type=F32)


def dot_t(a, b):
    return lax.dot_general(a, b, (((1,), (1,)), ((), ())), preferred_element_type=F32)


def aligned(index, size):
    return pl.ds(pl.multiple_of(index * size, size), size)


def only_head(pair, half):
    lane = lax.broadcasted_iota(jnp.int32, pair.shape, 1)
    return jnp.where((lane >= HEAD) == bool(half), pair, jnp.zeros_like(pair))


def pair_scores(queries, keys):
    both = jnp.concatenate([only_head(queries, 0), only_head(queries, 1)], axis=0)
    return dot_t(both, keys)


def lay_values(out, values):
    keys = values.shape[0]
    ones = jnp.ones_like(values)
    for half in range(2):
        rows = slice(half * keys, (half + 1) * keys)
        out[rows, :PAIR] = only_head(values, half)
        out[rows, PAIR:] = only_head(ones, half)


def weigh(scores, laid):
    rows = scores.shape[0] // 2
    parts = []
    for half in range(2):
        own = scores[half * rows : (half + 1) * rows]
        parts.append(jnp.exp2(own - jnp.max(own, axis=1, keepdims=True)).astype(BF16))
    mixed = dot(jnp.concatenate(parts, axis=1), laid)
    return mixed[:, :PAIR] / mixed[:, PAIR:]


def pipelined(items, first, second):
    held = first(items[0])
    for n, item in enumerate(items):
        now = held
        if n + 1 < len(items):
            held = first(items[n + 1])
        second(item, now)


def send_to(me, s, peers):
    return me ^ s if peers & (peers - 1) == 0 else (me + s) % peers


def got_from(me, s, peers):
    return me ^ s if peers & (peers - 1) == 0 else (me + peers - s) % peers


def start_all(copies):
    for copy in copies:
        copy.start()


def wait_all(copies):
    for copy in copies:
        copy.wait()


def feed_forward(y, gain2, gain3, up_s, down_s):
    inner = norm(y, gain2[...]).astype(BF16)
    total = [y.astype(F32)]

    def rise(c):
        return dot(inner, up_s[:, c * HIDE : (c + 1) * HIDE])

    def fall(c, got):
        total[0] = total[0] + dot(gelu(got).astype(BF16), down_s[c * HIDE : (c + 1) * HIDE, :])

    pipelined(list(range(up_s.shape[1] // HIDE)), rise, fall)
    z = total[0].astype(BF16)
    return z, norm(z, gain3[...]).astype(BF16)


def layer_one_kernel(peers, cap, *refs):
    pick_ref, ids, gain1, gain2, gain3, points, w_in, w_out, w_up, w_down = refs[:10]
    z_out, h_out = refs[10:12]
    sends, refs = refs[12 : 12 + peers], refs[12 + peers :]
    x_s, in_s, wo_s, up_s, down_s, q_s, k_s, v_s, bias_s, mix_s, y_s, z_s, h_s, p_s, sem, send_sem = refs
    me = lax.axis_index("pts").astype(jnp.int32)
    count, width = x_s.shape
    balls = count // BALL
    pairs = width // PAIR
    blocks = count // LEAF
    copies = [
        pltpu.make_async_copy(w_out, wo_s, sem.at[0]),
        pltpu.make_async_copy(w_up, up_s, sem.at[1]),
        pltpu.make_async_copy(w_down, down_s, sem.at[2]),
    ]
    thirds, balls_in = [], []
    for i in range(3):
        cols = pl.ds(i * width, width)
        thirds.append(pltpu.make_async_copy(w_in.at[:, cols], in_s.at[:, cols], sem.at[3 + i]))
    for b in range(balls):
        at = pl.ds(b * BALL, BALL)
        balls_in.append(pltpu.make_async_copy(points.at[at, :], x_s.at[at, :], sem.at[6 + 3 * b]))
    balls_in[0].start()
    start_all(thirds)
    start_all(balls_in[1:])
    for b in range(balls):
        across = jnp.broadcast_to(ids[b : b + 1, :], (LEAF, BALL)).astype(F32)
        down = across.T
        for c in range(BALL // LEAF):
            cols = slice(c * LEAF, (c + 1) * LEAF)
            bias_s[b, :, cols] = jnp.where(down == across[:1, cols], 0.0, -1e30)
    for b in range(balls):
        rows = slice(b * BALL, (b + 1) * BALL)
        balls_in[b].wait()
        h1 = norm(x_s[rows, :], gain1[...]).astype(BF16)

        def product(i):
            if b == 0:
                thirds[i].wait()
            return dot(h1, in_s[:, i * width : (i + 1) * width])

        q_s[rows, :] = (product(0) * SCALE).astype(BF16)
        k_s[rows, :] = product(1).astype(BF16)
        values = product(2).astype(BF16)
        if b == 0:
            start_all(copies)
        for g in range(pairs):
            lay_values(v_s.at[b * pairs + g], values[:, g * PAIR : (g + 1) * PAIR])

    def scores(item):
        b, g, c = item
        cols = slice(g * PAIR, (g + 1) * PAIR)
        at = b * BALL + c * CHUNK
        return pair_scores(q_s[at : at + CHUNK, cols], k_s[b * BALL : (b + 1) * BALL, cols])

    def mix(item, got):
        b, g, c = item
        at = b * BALL + c * CHUNK
        bias = bias_s[b, c * CHUNK : (c + 1) * CHUNK, :]
        out = weigh(got + jnp.concatenate([bias, bias], axis=0), v_s[b * pairs + g])
        mix_s[at : at + CHUNK, g * PAIR : (g + 1) * PAIR] = out.astype(BF16)

    pipelined(
        [(b, g, c) for b in range(balls) for g in range(pairs) for c in range(BALL // CHUNK)], scores, mix
    )
    copies[0].wait()
    for b in range(balls):
        rows = slice(b * BALL, (b + 1) * BALL)
        y_s[rows, :] = (x_s[rows, :].astype(F32) + dot(mix_s[rows, :], wo_s[...])).astype(BF16)
    copies[1].wait()
    copies[2].wait()
    outgoing, pooled = [], []
    for b in range(balls):
        rows = slice(b * BALL, (b + 1) * BALL)
        z, h3 = feed_forward(y_s[rows, :], gain2, gain3, up_s, down_s)
        z_s[rows, :] = z
        h_s[rows, :] = h3
        wide = h3.astype(F32)
        for c in range(BALL // CMP):
            pooled.append(jnp.sum(wide[c * CMP : (c + 1) * CMP], axis=0, keepdims=True) * CMP ** (-0.5))
        at = pl.ds(b * BALL, BALL)
        for n, (source, there) in enumerate(((z_s, z_out), (h_s, h_out))):
            copy = pltpu.make_async_copy(source.at[at, :], there.at[at, :], sem.at[7 + 3 * b + n])
            copy.start()
            outgoing.append(copy)
    row = lax.broadcasted_iota(jnp.int32, p_s.shape, 0)
    small = jnp.zeros(p_s.shape, F32)
    for i, part in enumerate(pooled):
        small = jnp.where(row == i, part, small)
    p_s[...] = small.astype(BF16)
    for s in range(peers - 1, -1, -1):
        there = sends[s].at[pl.ds(cap * LEAF, p_s.shape[0]), :]
        copy = pltpu.make_async_copy(p_s, there, send_sem.at[peers * cap + s])
        copy.start()
        outgoing.append(copy)
        for c in range(cap):
            slot = send_to(me, s, peers) * cap + c
            block = jnp.minimum(pick_ref[0, slot], blocks - 1)
            there = sends[s].at[pl.ds(c * LEAF, LEAF), :]
            copy = pltpu.make_async_copy(h_s.at[aligned(block, LEAF), :], there, send_sem.at[s * cap + c])
            copy.start()
            outgoing.append(copy)
    wait_all(outgoing)


def layer_one(peers, cap, pick, ids, gains, points, weights):
    count, width = points.shape
    hidden = weights[2].shape[1]
    whole = jax.ShapeDtypeStruct((count, width), BF16)
    tail = -(-(count // CMP) // TILE) * TILE
    block = jax.ShapeDtypeStruct((cap * LEAF + tail, width), BF16)
    balls = count // BALL
    return pl.pallas_call(
        partial(layer_one_kernel, peers, cap),
        out_shape=[whole, whole] + [block] * peers,
        in_specs=[SMEM] + [VMEM] * 4 + [ANY] * 5,
        out_specs=[ANY, ANY] + [ANY] * peers,
        scratch_shapes=[
            pltpu.VMEM((count, width), BF16),
            pltpu.VMEM((width, 3 * width), BF16),
            pltpu.VMEM((width, width), BF16),
            pltpu.VMEM((width, hidden), BF16),
            pltpu.VMEM((hidden, width), BF16),
            pltpu.VMEM((count, width), BF16),
            pltpu.VMEM((count, width), BF16),
            pltpu.VMEM((balls * width // PAIR, 2 * BALL, 2 * PAIR), BF16),
            pltpu.VMEM((balls, BALL, BALL), F32),
            pltpu.VMEM((count, width), BF16),
            pltpu.VMEM((count, width), BF16),
            pltpu.VMEM((count, width), BF16),
            pltpu.VMEM((count, width), BF16),
            pltpu.VMEM((tail, width), BF16),
            pltpu.SemaphoreType.DMA((6 + 3 * balls,)),
            pltpu.SemaphoreType.DMA((peers * (cap + 1),)),
        ],
        compiler_params=pltpu.CompilerParams(vmem_limit_bytes=60 * MIB),
        cost_estimate=pl.CostEstimate(
            flops=count * width * (8 * width + 4 * hidden + 16 * BALL),
            bytes_accessed=10 * MIB,
            transcendentals=count * BALL * width // HEAD,
        ),
        name="layer_one",
    )(pick, ids, *gains, points, *weights)


def place_of(recv_ref, slot, blocks):
    place, found = jnp.int32(0), jnp.int32(0)
    for j in range(blocks):
        hit = (recv_ref[0, j] == slot).astype(jnp.int32)
        place = place + j * hit
        found = found + hit
    return place, found > 0


def layer_two_kernel(peers, cap, flow, blocks, start, columns, *refs):
    recv_ref = refs[0]
    arrived = dict(zip(flow, refs[1 : 1 + peers]))
    w_in = refs[1 + peers]
    outs = refs[2 + peers : 2 + 2 * peers]
    h_s, q_s, k_s, v_s, a_s = refs[2 + 2 * peers :]
    width = h_s.shape[1]
    pairs = columns // PAIR
    me = lax.axis_index("pts").astype(jnp.int32)
    balls = blocks * LEAF // BALL
    places = []
    for s in range(peers):
        for c in range(cap):
            place, found = place_of(recv_ref, got_from(me, s, peers) * cap + c, blocks)
            places.append(place)

            @pl.when(found)
            def _():
                h_s[aligned(place, LEAF), :] = arrived[s][c * LEAF : (c + 1) * LEAF, :]

    def product(h, i):
        return dot(h, w_in[:, i * width + start : i * width + start + columns])

    for b in range(balls):
        rows = slice(b * BALL, (b + 1) * BALL)
        h = h_s[rows, :]
        q_s[rows, :] = (product(h, 0) * SCALE).astype(BF16)
        k_s[rows, :] = product(h, 1).astype(BF16)
        values = product(h, 2).astype(BF16)
        for g in range(pairs):
            lay_values(v_s.at[b * pairs + g], values[:, g * PAIR : (g + 1) * PAIR])

    def scores(item):
        b, g, c = item
        cols = slice(g * PAIR, (g + 1) * PAIR)
        at = b * BALL + c * CHUNK
        return pair_scores(q_s[at : at + CHUNK, cols], k_s[b * BALL : (b + 1) * BALL, cols])

    def mix(item, got):
        b, g, c = item
        at = b * BALL + c * CHUNK
        a_s[at : at + CHUNK, g * PAIR : (g + 1) * PAIR] = weigh(got, v_s[b * pairs + g]).astype(BF16)

    pipelined(
        [(b, g, c) for b in range(balls) for g in range(pairs) for c in range(BALL // CHUNK)], scores, mix
    )
    for s in range(peers):
        for c in range(cap):
            outs[s][c * LEAF : (c + 1) * LEAF, :] = a_s[aligned(places[s * cap + c], LEAF), :]


def layer_two(peers, cap, flow, start, columns, recv, arrived, w_in):
    blocks = recv.shape[1]
    width = w_in.shape[0]
    pairs = columns // PAIR
    rows = blocks * LEAF
    block = jax.ShapeDtypeStruct((cap * LEAF, columns), BF16)
    return pl.pallas_call(
        partial(layer_two_kernel, peers, cap, flow, blocks, start, columns),
        out_shape=[block] * peers,
        in_specs=[SMEM] + [VMEM] * (peers + 1),
        out_specs=[VMEM] * peers,
        scratch_shapes=[
            pltpu.VMEM((rows, width), BF16),
            pltpu.VMEM((rows, columns), BF16),
            pltpu.VMEM((rows, columns), BF16),
            pltpu.VMEM((rows // BALL * pairs, 2 * BALL, 2 * PAIR), BF16),
            pltpu.VMEM((rows, columns), BF16),
        ],
        compiler_params=pltpu.CompilerParams(vmem_limit_bytes=LATER),
        cost_estimate=pl.CostEstimate(
            flops=rows * columns * (6 * width + 16 * BALL),
            bytes_accessed=4 * MIB,
            transcendentals=rows * BALL * columns // HEAD,
        ),
        name=f"layer_two_{start}",
    )(recv, *[arrived[s] for s in flow], w_in)


def compressed_kernel(slabs, tail, local, *refs):
    pools = refs[:slabs]
    h, z, w_comp, w_in, w_out, out = refs[slabs : slabs + 6]
    h_s, z_s, p_s, wc_s, wq_s, wo_s, q_s, ck_s, cv_s, a_s, o_s, sem, pool_sem, out_sem = refs[slabs + 6 :]
    rows, width = h_s.shape
    pairs = width // PAIR
    comp = ck_s.shape[0]
    copies = [
        pltpu.make_async_copy(w_comp, wc_s, sem.at[0]),
        pltpu.make_async_copy(w_in.at[:, pl.ds(0, width)], wq_s, sem.at[1]),
        pltpu.make_async_copy(h, h_s, sem.at[2]),
        pltpu.make_async_copy(w_out, wo_s, sem.at[3]),
        pltpu.make_async_copy(z, z_s, sem.at[4]),
    ]
    small = []
    for n, pool in enumerate(pools):
        there = p_s.at[pl.ds(n * pool.shape[0], pool.shape[0]), :]
        small.append(pltpu.make_async_copy(pool, there, pool_sem.at[n]))
    start_all(small)
    start_all(copies)
    key = lax.broadcasted_iota(jnp.int32, (comp, p_s.shape[0]), 0)
    at = lax.broadcasted_iota(jnp.int32, (comp, p_s.shape[0]), 1)
    taken = jnp.where(at == key // local * tail + key % local, 1.0, 0.0).astype(BF16)
    wait_all(small)
    pooled = dot(taken, p_s[...]).astype(BF16)
    copies[0].wait()
    far = dot(pooled, wc_s[...]).astype(BF16)
    ck_s[...] = far[:, :width]
    for g in range(pairs):
        lay_values(cv_s.at[g], far[:, width + g * PAIR : width + (g + 1) * PAIR])
    wait_all(copies[1:3])
    q_s[...] = (dot(h_s[...], wq_s[...]) * SCALE).astype(BF16)

    def scores(item):
        g, c = item
        cols = slice(g * PAIR, (g + 1) * PAIR)
        return pair_scores(q_s[c * CHUNK : (c + 1) * CHUNK, cols], ck_s[:, cols])

    def mix(item, got):
        g, c = item
        a_s[c * CHUNK : (c + 1) * CHUNK, g * PAIR : (g + 1) * PAIR] = weigh(got, cv_s[g]).astype(BF16)

    pipelined([(g, c) for c in range(rows // CHUNK) for g in range(pairs)], scores, mix)
    wait_all(copies[3:])
    outgoing = []
    for c in range(rows // CHUNK):
        at = slice(c * CHUNK, (c + 1) * CHUNK)
        o_s[at, :] = z_s[at, :].astype(F32) + dot(a_s[at, :], wo_s[...])
        there = pl.ds(c * CHUNK, CHUNK)
        copy = pltpu.make_async_copy(o_s.at[there, :], out.at[there, :], out_sem.at[c])
        copy.start()
        outgoing.append(copy)
    wait_all(outgoing)


def compressed(tail, local, pools, h, z, w_comp, w_in, w_out):
    rows, width = h.shape
    held = sum(p.shape[0] for p in pools)
    comp = held // tail * local
    return pl.pallas_call(
        partial(compressed_kernel, len(pools), tail, local),
        out_shape=jax.ShapeDtypeStruct((rows, width), F32),
        in_specs=[ANY] * (5 + len(pools)),
        out_specs=ANY,
        scratch_shapes=[
            pltpu.VMEM((rows, width), BF16),
            pltpu.VMEM((rows, width), BF16),
            pltpu.VMEM((held, width), BF16),
            pltpu.VMEM((width, 2 * width), BF16),
            pltpu.VMEM((width, width), BF16),
            pltpu.VMEM((width, width), BF16),
            pltpu.VMEM((rows, width), BF16),
            pltpu.VMEM((comp, width), BF16),
            pltpu.VMEM((width // PAIR, 2 * comp, 2 * PAIR), BF16),
            pltpu.VMEM((rows, width), BF16),
            pltpu.VMEM((rows, width), F32),
            pltpu.SemaphoreType.DMA((5,)),
            pltpu.SemaphoreType.DMA((len(pools),)),
            pltpu.SemaphoreType.DMA((rows // CHUNK,)),
        ],
        compiler_params=pltpu.CompilerParams(vmem_limit_bytes=LATER),
        cost_estimate=pl.CostEstimate(
            flops=rows * width * (4 * width + 16 * comp),
            bytes_accessed=8 * MIB,
            transcendentals=rows * comp * width // HEAD,
        ),
        name="compressed",
    )(*pools, h, z, w_comp, w_in, w_out)


def final_kernel(peers, cap, bounds, pick_ref, *refs):
    parts = len(bounds)
    back = [refs[p * peers : (p + 1) * peers][::-1] for p in range(parts)]
    w_out, base, out, m_s, o_s, out_sem = refs[parts * peers :]
    blocks = base.shape[0] // LEAF
    me = lax.axis_index("pts").astype(jnp.int32)
    for p, (start, columns) in enumerate(bounds):
        for s in range(peers):
            for c in range(cap):
                block = pick_ref[0, send_to(me, s, peers) * cap + c]

                @pl.when(block < blocks)
                def _():
                    got = back[p][s][c * LEAF : (c + 1) * LEAF, :]
                    m_s[aligned(block, LEAF), start : start + columns] = got

    outgoing = []
    for b in range(base.shape[0] // CHUNK):
        rows = slice(b * CHUNK, (b + 1) * CHUNK)
        o_s[rows, :] = (base[rows, :] + dot(m_s[rows, :], w_out[...])).astype(BF16)
        at = pl.ds(b * CHUNK, CHUNK)
        copy = pltpu.make_async_copy(o_s.at[at, :], out.at[at, :], out_sem.at[b])
        copy.start()
        outgoing.append(copy)
    wait_all(outgoing)


def final(peers, cap, bounds, pick, back, w_out, base):
    rows, width = base.shape
    return pl.pallas_call(
        partial(final_kernel, peers, cap, bounds),
        out_shape=jax.ShapeDtypeStruct((rows, width), BF16),
        in_specs=[SMEM] + [VMEM] * (peers * len(bounds) + 2),
        out_specs=ANY,
        scratch_shapes=[
            pltpu.VMEM((rows, width), BF16),
            pltpu.VMEM((rows, width), BF16),
            pltpu.SemaphoreType.DMA((rows // CHUNK,)),
        ],
        compiler_params=pltpu.CompilerParams(vmem_limit_bytes=LATER),
        cost_estimate=pl.CostEstimate(
            flops=2 * rows * width * width, bytes_accessed=4 * MIB, transcendentals=0
        ),
        name="last_product",
    )(pick, *back, w_out, base)


def shards(
    axes,
    points,
    ball_ids,
    send_pick,
    recv_from,
    gain_one,
    attn_in_one,
    attn_out_one,
    gain_two,
    mlp_up,
    mlp_down,
    gain_three,
    compress_proj,
    attn_in_two,
    attn_out_two,
):
    peers = axes[1][1]
    cap = send_pick.shape[1] // peers
    width = points.shape[1]
    gains = tuple(g.reshape(1, -1) for g in (gain_one, gain_two, gain_three))
    weights = (attn_in_one, attn_out_one, mlp_up, mlp_down)

    def travel(blocks, s, home):
        if s == 0:
            return blocks
        pattern = [(i, send_to(i, s, peers)) for i in range(peers)]
        if home:
            pattern = [(b, a) for a, b in pattern]
        return lax.ppermute(blocks, "pts", pattern)

    z, h, *sends = layer_one(peers, cap, send_pick, ball_ids, gains, points, weights)
    sends[0] = jnp.where(recv_from[0, 0] >= 0, sends[0], jnp.zeros_like(sends[0]))
    arrived = [travel(sends[s], s, False) for s in range(peers)]
    flow = [*range(peers - 1, 4, -1), *(s for s in (2, 1, 4, 3, 0) if s < peers)]
    tail = sends[0].shape[0] - cap * LEAF
    first = [s for s in (1, 2, 3, 0) if s < peers]
    last = list(range(peers - 1, 3, -1))
    slab = jnp.concatenate([arrived[s][cap * LEAF :] for s in first + last])
    groups = axes[0][1]
    doubles = groups & (groups - 1) == 0
    turns = [[(i, i ^ 1) for i in range(groups)]] if doubles and groups > 1 else []
    if not doubles:
        turns = [[(i, (i + s) % groups) for i in range(groups)] for s in range(1, groups)]
    pools = [slab] + [lax.ppermute(slab, "grp", turn) for turn in turns]
    mixed = layer_two(peers, cap, flow, 0, width, recv_from, arrived, attn_in_two)
    mixed, pools = lax.optimization_barrier((mixed, pools))
    bounds = [(0, width)]
    back = [travel(mixed[s], s, True) for s in range(peers - 1, -1, -1)]
    bit = 2
    while doubles and bit < groups:
        both = jnp.concatenate(pools)
        pools = [both, lax.ppermute(both, "grp", [(i, i ^ bit) for i in range(groups)])]
        bit *= 2
    local = points.shape[0] // CMP
    base = compressed(tail, local, pools, h, z, compress_proj, attn_in_two, attn_out_two)
    return final(peers, cap, bounds, send_pick, back, attn_out_two, base)


def solution(mesh):
    rows = P(("grp", "pts"), None)
    axes = (("grp", mesh.shape["grp"]), ("pts", mesh.shape["pts"]))
    return jax.shard_map(
        partial(shards, axes),
        mesh=mesh,
        in_specs=(rows,) * 4 + (P(),) * 10,
        out_specs=rows,
        check_vma=False,
    )
```

```python
from functools import partial
import math

import jax
import jax.numpy as jnp
from jax import lax
from jax.experimental import pallas as pl
from jax.experimental.pallas import tpu as pltpu
from jax.sharding import PartitionSpec as P

HEAD = 64
LEAF = 128
BALL = 512
CMP = 256
PAIR = 2 * HEAD
HIDE = 512
CHUNK = 256
TILE = 16
MIB = 1 << 20
LATER = 40 * MIB
F32 = jnp.float32
BF16 = jnp.bfloat16
SCALE = HEAD ** (-0.5) * math.log2(math.e)

ANY = pl.BlockSpec(memory_space=pl.ANY)
VMEM = pl.BlockSpec(memory_space=pltpu.VMEM)
SMEM = pl.BlockSpec(memory_space=pltpu.SMEM)


def norm(values, gain):
    wide = values.astype(F32)
    return wide * lax.rsqrt(jnp.mean(wide * wide, axis=-1, keepdims=True) + 1e-06) * gain


def gelu(x):
    c = math.sqrt(2.0 / math.pi)
    t = jnp.tanh(x * (c + (c * 0.044715) * (x * x)))
    return x * (0.5 + 0.5 * t)


def dot(a, b):
    return jnp.dot(a, b, preferred_element_type=F32)


def dot_t(a, b):
    return lax.dot_general(a, b, (((1,), (1,)), ((), ())), preferred_element_type=F32)


def aligned(index, size):
    return pl.ds(pl.multiple_of(index * size, size), size)


def only_head(pair, half):
    lane = lax.broadcasted_iota(jnp.int32, pair.shape, 1)
    return jnp.where((lane >= HEAD) == bool(half), pair, jnp.zeros_like(pair))


def pair_scores(queries, keys):
    both = jnp.concatenate([only_head(queries, 0), only_head(queries, 1)], axis=0)
    return dot_t(both, keys)


def lay_values(out, values):
    keys = values.shape[0]
    ones = jnp.ones_like(values)
    for half in range(2):
        rows = slice(half * keys, (half + 1) * keys)
        out[rows, :PAIR] = only_head(values, half)
        out[rows, PAIR:] = only_head(ones, half)


def weigh(scores, laid):
    rows = scores.shape[0] // 2
    parts = []
    for half in range(2):
        own = scores[half * rows : (half + 1) * rows]
        parts.append(jnp.exp2(own - jnp.max(own, axis=1, keepdims=True)).astype(BF16))
    mixed = dot(jnp.concatenate(parts, axis=1), laid)
    return mixed[:, :PAIR] / mixed[:, PAIR:]


def pipelined(items, first, second):
    held = first(items[0])
    for n, item in enumerate(items):
        now = held
        if n + 1 < len(items):
            held = first(items[n + 1])
        second(item, now)


def send_to(me, s, peers):
    return me ^ s if peers & (peers - 1) == 0 else (me + s) % peers


def got_from(me, s, peers):
    return me ^ s if peers & (peers - 1) == 0 else (me + peers - s) % peers


def start_all(copies):
    for copy in copies:
        copy.start()


def wait_all(copies):
    for copy in copies:
        copy.wait()


def feed_forward(y, gain2, gain3, up_s, down_s):
    inner = norm(y, gain2[...]).astype(BF16)
    total = [y.astype(F32)]

    def rise(c):
        return dot(inner, up_s[:, c * HIDE : (c + 1) * HIDE])

    def fall(c, got):
        total[0] = total[0] + dot(gelu(got).astype(BF16), down_s[c * HIDE : (c + 1) * HIDE, :])

    pipelined(list(range(up_s.shape[1] // HIDE)), rise, fall)
    z = total[0].astype(BF16)
    return z, norm(z, gain3[...]).astype(BF16)


def layer_one_kernel(peers, cap, *refs):
    pick_ref, ids, gain1, gain2, gain3, points, w_in, w_out, w_up, w_down = refs[:10]
    z_out, h_out = refs[10:12]
    sends, refs = refs[12 : 12 + peers], refs[12 + peers :]
    x_s, in_s, wo_s, up_s, down_s, q_s, k_s, v_s, bias_s, mix_s, y_s, z_s, h_s, p_s, sem, send_sem = refs
    me = lax.axis_index("pts").astype(jnp.int32)
    count, width = x_s.shape
    balls = count // BALL
    pairs = width // PAIR
    blocks = count // LEAF
    copies = [
        pltpu.make_async_copy(w_out, wo_s, sem.at[0]),
        pltpu.make_async_copy(w_up, up_s, sem.at[1]),
        pltpu.make_async_copy(w_down, down_s, sem.at[2]),
    ]
    thirds, balls_in = [], []
    for i in range(3):
        cols = pl.ds(i * width, width)
        thirds.append(pltpu.make_async_copy(w_in.at[:, cols], in_s.at[:, cols], sem.at[3 + i]))
    for b in range(balls):
        at = pl.ds(b * BALL, BALL)
        balls_in.append(pltpu.make_async_copy(points.at[at, :], x_s.at[at, :], sem.at[6 + 3 * b]))
    balls_in[0].start()
    start_all(thirds)
    start_all(balls_in[1:])
    for b in range(balls):
        across = jnp.broadcast_to(ids[b : b + 1, :], (LEAF, BALL)).astype(F32)
        down = across.T
        for c in range(BALL // LEAF):
            cols = slice(c * LEAF, (c + 1) * LEAF)
            bias_s[b, :, cols] = jnp.where(down == across[:1, cols], 0.0, -1e30)
    for b in range(balls):
        rows = slice(b * BALL, (b + 1) * BALL)
        balls_in[b].wait()
        h1 = norm(x_s[rows, :], gain1[...]).astype(BF16)

        def product(i):
            if b == 0:
                thirds[i].wait()
            return dot(h1, in_s[:, i * width : (i + 1) * width])

        q_s[rows, :] = (product(0) * SCALE).astype(BF16)
        k_s[rows, :] = product(1).astype(BF16)
        values = product(2).astype(BF16)
        if b == 0:
            start_all(copies)
        for g in range(pairs):
            lay_values(v_s.at[b * pairs + g], values[:, g * PAIR : (g + 1) * PAIR])

    def scores(item):
        b, g, c = item
        cols = slice(g * PAIR, (g + 1) * PAIR)
        at = b * BALL + c * CHUNK
        return pair_scores(q_s[at : at + CHUNK, cols], k_s[b * BALL : (b + 1) * BALL, cols])

    def mix(item, got):
        b, g, c = item
        at = b * BALL + c * CHUNK
        bias = bias_s[b, c * CHUNK : (c + 1) * CHUNK, :]
        out = weigh(got + jnp.concatenate([bias, bias], axis=0), v_s[b * pairs + g])
        mix_s[at : at + CHUNK, g * PAIR : (g + 1) * PAIR] = out.astype(BF16)

    pipelined(
        [(b, g, c) for b in range(balls) for g in range(pairs) for c in range(BALL // CHUNK)], scores, mix
    )
    copies[0].wait()
    for b in range(balls):
        rows = slice(b * BALL, (b + 1) * BALL)
        y_s[rows, :] = (x_s[rows, :].astype(F32) + dot(mix_s[rows, :], wo_s[...])).astype(BF16)
    copies[1].wait()
    copies[2].wait()
    outgoing, pooled = [], []
    for b in range(balls):
        rows = slice(b * BALL, (b + 1) * BALL)
        z, h3 = feed_forward(y_s[rows, :], gain2, gain3, up_s, down_s)
        z_s[rows, :] = z
        h_s[rows, :] = h3
        wide = h3.astype(F32)
        for c in range(BALL // CMP):
            pooled.append(jnp.sum(wide[c * CMP : (c + 1) * CMP], axis=0, keepdims=True) * CMP ** (-0.5))
        at = pl.ds(b * BALL, BALL)
        for n, (source, there) in enumerate(((z_s, z_out), (h_s, h_out))):
            copy = pltpu.make_async_copy(source.at[at, :], there.at[at, :], sem.at[7 + 3 * b + n])
            copy.start()
            outgoing.append(copy)
    row = lax.broadcasted_iota(jnp.int32, p_s.shape, 0)
    small = jnp.zeros(p_s.shape, F32)
    for i, part in enumerate(pooled):
        small = jnp.where(row == i, part, small)
    p_s[...] = small.astype(BF16)
    for s in range(peers - 1, -1, -1):
        there = sends[s].at[pl.ds(cap * LEAF, p_s.shape[0]), :]
        copy = pltpu.make_async_copy(p_s, there, send_sem.at[peers * cap + s])
        copy.start()
        outgoing.append(copy)
        for c in range(cap):
            slot = send_to(me, s, peers) * cap + c
            block = jnp.minimum(pick_ref[0, slot], blocks - 1)
            there = sends[s].at[pl.ds(c * LEAF, LEAF), :]
            copy = pltpu.make_async_copy(h_s.at[aligned(block, LEAF), :], there, send_sem.at[s * cap + c])
            copy.start()
            outgoing.append(copy)
    wait_all(outgoing)


def layer_one(peers, cap, pick, ids, gains, points, weights):
    count, width = points.shape
    hidden = weights[2].shape[1]
    whole = jax.ShapeDtypeStruct((count, width), BF16)
    tail = -(-(count // CMP) // TILE) * TILE
    block = jax.ShapeDtypeStruct((cap * LEAF + tail, width), BF16)
    balls = count // BALL
    return pl.pallas_call(
        partial(layer_one_kernel, peers, cap),
        out_shape=[whole, whole] + [block] * peers,
        in_specs=[SMEM] + [VMEM] * 4 + [ANY] * 5,
        out_specs=[ANY, ANY] + [ANY] * peers,
        scratch_shapes=[
            pltpu.VMEM((count, width), BF16),
            pltpu.VMEM((width, 3 * width), BF16),
            pltpu.VMEM((width, width), BF16),
            pltpu.VMEM((width, hidden), BF16),
            pltpu.VMEM((hidden, width), BF16),
            pltpu.VMEM((count, width), BF16),
            pltpu.VMEM((count, width), BF16),
            pltpu.VMEM((balls * width // PAIR, 2 * BALL, 2 * PAIR), BF16),
            pltpu.VMEM((balls, BALL, BALL), F32),
            pltpu.VMEM((count, width), BF16),
            pltpu.VMEM((count, width), BF16),
            pltpu.VMEM((count, width), BF16),
            pltpu.VMEM((count, width), BF16),
            pltpu.VMEM((tail, width), BF16),
            pltpu.SemaphoreType.DMA((6 + 3 * balls,)),
            pltpu.SemaphoreType.DMA((peers * (cap + 1),)),
        ],
        compiler_params=pltpu.CompilerParams(vmem_limit_bytes=60 * MIB),
        cost_estimate=pl.CostEstimate(
            flops=count * width * (8 * width + 4 * hidden + 16 * BALL),
            bytes_accessed=10 * MIB,
            transcendentals=count * BALL * width // HEAD,
        ),
        name="layer_one",
    )(pick, ids, *gains, points, *weights)


def place_of(recv_ref, slot, blocks):
    place, found = jnp.int32(0), jnp.int32(0)
    for j in range(blocks):
        hit = (recv_ref[0, j] == slot).astype(jnp.int32)
        place = place + j * hit
        found = found + hit
    return place, found > 0


def layer_two_kernel(peers, cap, flow, blocks, start, columns, *refs):
    recv_ref = refs[0]
    arrived = dict(zip(flow, refs[1 : 1 + peers]))
    w_in = refs[1 + peers]
    outs = refs[2 + peers : 2 + 2 * peers]
    h_s, q_s, k_s, v_s, a_s = refs[2 + 2 * peers :]
    width = h_s.shape[1]
    pairs = columns // PAIR
    me = lax.axis_index("pts").astype(jnp.int32)
    balls = blocks * LEAF // BALL
    places = []
    for s in range(peers):
        for c in range(cap):
            place, found = place_of(recv_ref, got_from(me, s, peers) * cap + c, blocks)
            places.append(place)

            @pl.when(found)
            def _():
                h_s[aligned(place, LEAF), :] = arrived[s][c * LEAF : (c + 1) * LEAF, :]

    def product(h, i):
        return dot(h, w_in[:, i * width + start : i * width + start + columns])

    for b in range(balls):
        rows = slice(b * BALL, (b + 1) * BALL)
        h = h_s[rows, :]
        q_s[rows, :] = (product(h, 0) * SCALE).astype(BF16)
        k_s[rows, :] = product(h, 1).astype(BF16)
        values = product(h, 2).astype(BF16)
        for g in range(pairs):
            lay_values(v_s.at[b * pairs + g], values[:, g * PAIR : (g + 1) * PAIR])

    def scores(item):
        b, g, c = item
        cols = slice(g * PAIR, (g + 1) * PAIR)
        at = b * BALL + c * CHUNK
        return pair_scores(q_s[at : at + CHUNK, cols], k_s[b * BALL : (b + 1) * BALL, cols])

    def mix(item, got):
        b, g, c = item
        at = b * BALL + c * CHUNK
        a_s[at : at + CHUNK, g * PAIR : (g + 1) * PAIR] = weigh(got, v_s[b * pairs + g]).astype(BF16)

    pipelined(
        [(b, g, c) for b in range(balls) for g in range(pairs) for c in range(BALL // CHUNK)], scores, mix
    )
    for s in range(peers):
        for c in range(cap):
            outs[s][c * LEAF : (c + 1) * LEAF, :] = a_s[aligned(places[s * cap + c], LEAF), :]


def layer_two(peers, cap, flow, start, columns, recv, arrived, w_in):
    blocks = recv.shape[1]
    width = w_in.shape[0]
    pairs = columns // PAIR
    rows = blocks * LEAF
    block = jax.ShapeDtypeStruct((cap * LEAF, columns), BF16)
    return pl.pallas_call(
        partial(layer_two_kernel, peers, cap, flow, blocks, start, columns),
        out_shape=[block] * peers,
        in_specs=[SMEM] + [VMEM] * (peers + 1),
        out_specs=[VMEM] * peers,
        scratch_shapes=[
            pltpu.VMEM((rows, width), BF16),
            pltpu.VMEM((rows, columns), BF16),
            pltpu.VMEM((rows, columns), BF16),
            pltpu.VMEM((rows // BALL * pairs, 2 * BALL, 2 * PAIR), BF16),
            pltpu.VMEM((rows, columns), BF16),
        ],
        compiler_params=pltpu.CompilerParams(vmem_limit_bytes=LATER),
        cost_estimate=pl.CostEstimate(
            flops=rows * columns * (6 * width + 16 * BALL),
            bytes_accessed=4 * MIB,
            transcendentals=rows * BALL * columns // HEAD,
        ),
        name=f"layer_two_{start}",
    )(recv, *[arrived[s] for s in flow], w_in)


def compressed_kernel(slabs, tail, local, *refs):
    pools = refs[:slabs]
    h, z, w_comp, w_in, w_out, out = refs[slabs : slabs + 6]
    h_s, z_s, p_s, wc_s, wq_s, wo_s, q_s, ck_s, cv_s, a_s, o_s, sem, pool_sem, out_sem = refs[slabs + 6 :]
    rows, width = h_s.shape
    pairs = width // PAIR
    comp = ck_s.shape[0]
    copies = [
        pltpu.make_async_copy(w_comp, wc_s, sem.at[0]),
        pltpu.make_async_copy(w_in.at[:, pl.ds(0, width)], wq_s, sem.at[1]),
        pltpu.make_async_copy(h, h_s, sem.at[2]),
        pltpu.make_async_copy(w_out, wo_s, sem.at[3]),
        pltpu.make_async_copy(z, z_s, sem.at[4]),
    ]
    small = []
    for n, pool in enumerate(pools):
        there = p_s.at[pl.ds(n * pool.shape[0], pool.shape[0]), :]
        small.append(pltpu.make_async_copy(pool, there, pool_sem.at[n]))
    start_all(small)
    start_all(copies)
    key = lax.broadcasted_iota(jnp.int32, (comp, p_s.shape[0]), 0)
    at = lax.broadcasted_iota(jnp.int32, (comp, p_s.shape[0]), 1)
    taken = jnp.where(at == key // local * tail + key % local, 1.0, 0.0).astype(BF16)
    wait_all(small)
    pooled = dot(taken, p_s[...]).astype(BF16)
    copies[0].wait()
    far = dot(pooled, wc_s[...]).astype(BF16)
    ck_s[...] = far[:, :width]
    for g in range(pairs):
        lay_values(cv_s.at[g], far[:, width + g * PAIR : width + (g + 1) * PAIR])
    wait_all(copies[1:3])
    q_s[...] = (dot(h_s[...], wq_s[...]) * SCALE).astype(BF16)

    def scores(item):
        g, c = item
        cols = slice(g * PAIR, (g + 1) * PAIR)
        return pair_scores(q_s[c * CHUNK : (c + 1) * CHUNK, cols], ck_s[:, cols])

    def mix(item, got):
        g, c = item
        a_s[c * CHUNK : (c + 1) * CHUNK, g * PAIR : (g + 1) * PAIR] = weigh(got, cv_s[g]).astype(BF16)

    pipelined([(g, c) for c in range(rows // CHUNK) for g in range(pairs)], scores, mix)
    wait_all(copies[3:])
    outgoing = []
    for c in range(rows // CHUNK):
        at = slice(c * CHUNK, (c + 1) * CHUNK)
        o_s[at, :] = z_s[at, :].astype(F32) + dot(a_s[at, :], wo_s[...])
        there = pl.ds(c * CHUNK, CHUNK)
        copy = pltpu.make_async_copy(o_s.at[there, :], out.at[there, :], out_sem.at[c])
        copy.start()
        outgoing.append(copy)
    wait_all(outgoing)


def compressed(tail, local, pools, h, z, w_comp, w_in, w_out):
    rows, width = h.shape
    held = sum(p.shape[0] for p in pools)
    comp = held // tail * local
    return pl.pallas_call(
        partial(compressed_kernel, len(pools), tail, local),
        out_shape=jax.ShapeDtypeStruct((rows, width), F32),
        in_specs=[ANY] * (5 + len(pools)),
        out_specs=ANY,
        scratch_shapes=[
            pltpu.VMEM((rows, width), BF16),
            pltpu.VMEM((rows, width), BF16),
            pltpu.VMEM((held, width), BF16),
            pltpu.VMEM((width, 2 * width), BF16),
            pltpu.VMEM((width, width), BF16),
            pltpu.VMEM((width, width), BF16),
            pltpu.VMEM((rows, width), BF16),
            pltpu.VMEM((comp, width), BF16),
            pltpu.VMEM((width // PAIR, 2 * comp, 2 * PAIR), BF16),
            pltpu.VMEM((rows, width), BF16),
            pltpu.VMEM((rows, width), F32),
            pltpu.SemaphoreType.DMA((5,)),
            pltpu.SemaphoreType.DMA((len(pools),)),
            pltpu.SemaphoreType.DMA((rows // CHUNK,)),
        ],
        compiler_params=pltpu.CompilerParams(vmem_limit_bytes=LATER),
        cost_estimate=pl.CostEstimate(
            flops=rows * width * (4 * width + 16 * comp),
            bytes_accessed=8 * MIB,
            transcendentals=rows * comp * width // HEAD,
        ),
        name="compressed",
    )(*pools, h, z, w_comp, w_in, w_out)


def final_kernel(peers, cap, flow, bounds, pick_ref, *refs):
    parts = len(bounds)
    back = [dict(zip(flow, refs[p * peers : (p + 1) * peers])) for p in range(parts)]
    w_out, base, out, m_s, o_s, out_sem = refs[parts * peers :]
    blocks = base.shape[0] // LEAF
    me = lax.axis_index("pts").astype(jnp.int32)
    for p, (start, columns) in enumerate(bounds):
        for s in range(peers):
            for c in range(cap):
                block = pick_ref[0, send_to(me, s, peers) * cap + c]

                @pl.when(block < blocks)
                def _():
                    got = back[p][s][c * LEAF : (c + 1) * LEAF, :]
                    m_s[aligned(block, LEAF), start : start + columns] = got

    outgoing = []
    for b in range(base.shape[0] // CHUNK):
        rows = slice(b * CHUNK, (b + 1) * CHUNK)
        o_s[rows, :] = (base[rows, :] + dot(m_s[rows, :], w_out[...])).astype(BF16)
        at = pl.ds(b * CHUNK, CHUNK)
        copy = pltpu.make_async_copy(o_s.at[at, :], out.at[at, :], out_sem.at[b])
        copy.start()
        outgoing.append(copy)
    wait_all(outgoing)


def final(peers, cap, flow, bounds, pick, back, w_out, base):
    rows, width = base.shape
    return pl.pallas_call(
        partial(final_kernel, peers, cap, flow, bounds),
        out_shape=jax.ShapeDtypeStruct((rows, width), BF16),
        in_specs=[SMEM] + [VMEM] * (peers * len(bounds) + 2),
        out_specs=ANY,
        scratch_shapes=[
            pltpu.VMEM((rows, width), BF16),
            pltpu.VMEM((rows, width), BF16),
            pltpu.SemaphoreType.DMA((rows // CHUNK,)),
        ],
        compiler_params=pltpu.CompilerParams(vmem_limit_bytes=LATER),
        cost_estimate=pl.CostEstimate(
            flops=2 * rows * width * width, bytes_accessed=4 * MIB, transcendentals=0
        ),
        name="last_product",
    )(pick, *back, w_out, base)


def shards(
    axes,
    points,
    ball_ids,
    send_pick,
    recv_from,
    gain_one,
    attn_in_one,
    attn_out_one,
    gain_two,
    mlp_up,
    mlp_down,
    gain_three,
    compress_proj,
    attn_in_two,
    attn_out_two,
):
    peers = axes[1][1]
    cap = send_pick.shape[1] // peers
    width = points.shape[1]
    gains = tuple(g.reshape(1, -1) for g in (gain_one, gain_two, gain_three))
    weights = (attn_in_one, attn_out_one, mlp_up, mlp_down)

    def travel(blocks, s, home):
        if s == 0:
            return blocks
        pattern = [(i, send_to(i, s, peers)) for i in range(peers)]
        if home:
            pattern = [(b, a) for a, b in pattern]
        return lax.ppermute(blocks, "pts", pattern)

    z, h, *sends = layer_one(peers, cap, send_pick, ball_ids, gains, points, weights)
    sends[0] = jnp.where(recv_from[0, 0] >= 0, sends[0], jnp.zeros_like(sends[0]))
    arrived = [travel(sends[s], s, False) for s in range(peers)]
    flow = [*range(peers - 1, 5, -1), *(s for s in (3, 2, 1, 5, 4, 0) if s < peers)]
    home = [*range(peers - 1, 4, -1), *(s for s in (2, 1, 4, 3, 0) if s < peers)]
    tail = sends[0].shape[0] - cap * LEAF
    first = [s for s in (1, 2, 3, 0) if s < peers]
    last = list(range(peers - 1, 3, -1))
    slab = jnp.concatenate([arrived[s][cap * LEAF :] for s in first + last])
    groups = axes[0][1]
    doubles = groups & (groups - 1) == 0
    turns = [[(i, i ^ 1) for i in range(groups)]] if doubles and groups > 1 else []
    if not doubles:
        turns = [[(i, (i + s) % groups) for i in range(groups)] for s in range(1, groups)]
    pools = [slab] + [lax.ppermute(slab, "grp", turn) for turn in turns]
    mixed = layer_two(peers, cap, flow, 0, width, recv_from, arrived, attn_in_two)
    mixed, pools = lax.optimization_barrier((mixed, pools))
    bounds = [(0, width)]
    back = {s: travel(mixed[s], s, True) for s in home}
    bit = 2
    while doubles and bit < groups:
        both = jnp.concatenate(pools)
        pools = [both, lax.ppermute(both, "grp", [(i, i ^ bit) for i in range(groups)])]
        bit *= 2
    local = points.shape[0] // CMP
    soon = [back[s] for s in (1, 2) if s < peers]
    z, soon = lax.optimization_barrier((z, soon))
    back.update(zip((1, 2), soon))
    base = compressed(tail, local, pools, h, z, compress_proj, attn_in_two, attn_out_two)
    return final(peers, cap, home, bounds, send_pick, [back[s] for s in home], attn_out_two, base)


def solution(mesh):
    rows = P(("grp", "pts"), None)
    axes = (("grp", mesh.shape["grp"]), ("pts", mesh.shape["pts"]))
    return jax.shard_map(
        partial(shards, axes),
        mesh=mesh,
        in_specs=(rows,) * 4 + (P(),) * 10,
        out_specs=rows,
        check_vma=False,
    )
```
